512 devices in a mesh: genome: 128 (over y, z, core), rep: 4 (over x).
Axes of the slice: x: 4, y: 8, z: 8, core: 2. Of those that a mesh axis runs over, the one named last changes fastest.
Arguments:
- band_tiles: float32 [1024, 5, 256, 256], P(('genome', 'rep'))
- trans_tiles: float32 [3072, 256, 256], P(('genome', 'rep'))
- trans_rows: int32 [3072], P(('genome', 'rep')), may hold values from 0 to 1023
- trans_cols: int32 [3072], P(('genome', 'rep')), may hold values from 0 to 1023
- trans_count: int32 [512], P(('genome', 'rep')), may hold values from 0 to 6, as said below
- masked: int32 [262144], P('genome'), may hold values 0 or 1
Outputs:
- weights: float32 [262144], P('genome')
- coverage: float32 [262144], P('genome')
The draws below stay inside these ranges and needn't reach their ends.
Inputs may be any that keep to these rules, and one draw needn't show every extreme that they name: `trans_count`: for device d = g * 4 + r, its used slots have row blocks within g * 8 to (g + 1) * 8 - 1 and column blocks on distinct genome indices of g + 2 or more; the device g = 0, r = 0 uses all 6 slots.
All inputs are finite; a program needn't handle non-finite values. No bound on the sum of `masked` on one device may be relied on, other than what follows from the above.
Results may differ from the reference program's by a relative error of at most 0.00012.
Values sent between devices are 32-bit elements; how exact they have to be, the bound alone decides.
No kernel may reach another device: no remote copies, remote signals or barrier semaphores. Data moves between devices by JAX's collectives and lax.ppermute only.
A program may use at most 128 MiB of HBM per device.

```python
import jax
import jax.numpy as jnp
from jax import lax

TILE = 256
BAND = 4
TRANS_DEV = 6
ITERS = 2
BLK_G = 8
NB = 1024
BINS = 262144
DEVICES = 512


def layout(key):
    key = jax.random.fold_in(key, 11)
    groups = NB // BLK_G
    replicas = DEVICES // groups
    device_ids = jnp.arange(DEVICES, dtype=jnp.int32)
    keys = jax.random.split(key, DEVICES)

    def one_device(dkey, device):
        genome_at = device // replicas
        replica_at = device % replicas
        perm_key, count_key, row_key, col_key = jax.random.split(dkey, 4)
        owner_ids = jnp.arange(groups, dtype=jnp.int32)
        scores = jax.random.permutation(perm_key, groups).astype(jnp.int32)
        scores = jnp.where(owner_ids >= genome_at + 2, scores, groups + owner_ids)
        chosen = jnp.argsort(scores, stable=True)[:TRANS_DEV].astype(jnp.int32)
        avail = jnp.maximum(groups - genome_at - 2, 0)
        wanted = jax.random.randint(count_key, (), TRANS_DEV // 2, TRANS_DEV + 1)
        wanted = jnp.where(replica_at == 0, TRANS_DEV, wanted)
        count = jnp.minimum(wanted, avail).astype(jnp.int32)
        rows = genome_at * BLK_G + jax.random.randint(row_key, (TRANS_DEV,), 0, BLK_G)
        cols = chosen * BLK_G + jax.random.randint(col_key, (TRANS_DEV,), 0, BLK_G)
        return (rows.astype(jnp.int32), cols.astype(jnp.int32), count)
    rows, cols, counts = jax.vmap(one_device)(keys, device_ids)
    return (rows.reshape(-1), cols.reshape(-1), counts)


def visibility(key, low, high):
    key = jax.random.fold_in(key, 12)
    return jnp.exp(jax.random.uniform(key, (NB, TILE), jnp.float32, jnp.log(low), jnp.log(high)))


def draw_band_tiles(key, part):
    seen = visibility(key, 0.3, 3.0)
    key = jax.random.fold_in(key, 3)
    noise = jnp.exp(jax.random.uniform(key, (NB, BAND + 1, TILE, TILE), jnp.float32, jnp.log(0.5), jnp.log(2.0)))
    reach = (jnp.arange(NB)[:, None] + jnp.arange(BAND + 1)[None, :]) % NB
    decay = 1.0 / (1.0 + jnp.arange(BAND + 1, dtype=jnp.float32))
    tiles = seen[:, None, :, None] * seen[reach][:, :, None, :] * noise * decay[None, :, None, None]
    return tiles.astype(jnp.float32)


def draw_trans_tiles(key, part):
    rows, cols, counts = layout(key)
    seen = visibility(key, 0.3, 3.0)
    key = jax.random.fold_in(key, 4)
    noise = jnp.exp(jax.random.uniform(key, (DEVICES * TRANS_DEV, TILE, TILE), jnp.float32, jnp.log(0.2), jnp.log(1.0)))
    return (seen[rows][:, :, None] * seen[cols][:, None, :] * noise).astype(jnp.float32)


def draw_trans_rows(key, part):
    return layout(key)[0]


def draw_trans_cols(key, part):
    return layout(key)[1]


def draw_trans_count(key, part):
    return layout(key)[2]


def with_ends(result, rng, smallest, high):
    index_at = [jax.random.randint(jax.random.fold_in(rng, axis), (), 0, length) for axis, length in enumerate(result.shape)]
    main_axis = result.shape.index(max(result.shape))
    next_to = index_at[:main_axis] + [(index_at[main_axis] + 1) % result.shape[main_axis]] + index_at[main_axis + 1:]
    return result.at[tuple(index_at)].set(smallest).at[tuple(next_to)].set(high)


def setup_inputs(seed: int = 0) -> dict:
    streams_of = jax.random.split(jax.random.key(seed), 7)
    band_tiles = draw_band_tiles(jax.random.fold_in(streams_of[6], 71), 0)
    trans_tiles = draw_trans_tiles(jax.random.fold_in(streams_of[6], 71), 0)
    trans_rows = draw_trans_rows(jax.random.fold_in(streams_of[6], 71), 0)
    trans_cols = draw_trans_cols(jax.random.fold_in(streams_of[6], 71), 0)
    trans_count = draw_trans_count(jax.random.fold_in(streams_of[6], 71), 0)
    masked = with_ends((jax.random.randint(streams_of[5], (BINS,), 0, 10) < 1).astype(jnp.int32), jax.random.fold_in(streams_of[5], 1), 0, 1)
    return {"band_tiles": band_tiles, "trans_tiles": trans_tiles, "trans_rows": trans_rows, "trans_cols": trans_cols, "trans_count": trans_count, "masked": masked}


HIGH = lax.Precision.HIGHEST


def reference(band_tiles, trans_tiles, trans_rows, trans_cols, trans_count, masked):
    unmasked = (1 - masked).astype(jnp.float32).reshape(NB, TILE)
    upper = jnp.triu(jnp.ones((TILE, TILE), jnp.float32))
    offset_ids = jnp.arange(BAND + 1)
    shape_mask = jnp.where(offset_ids[:, None, None] == 0, upper[None], jnp.ones((1, TILE, TILE), jnp.float32))
    slot_ids = jnp.arange(TRANS_DEV, dtype=jnp.int32)
    active = (slot_ids[None, :] < trans_count[:, None]).reshape(-1).astype(jnp.float32)
    weights = unmasked
    coverage = unmasked
    for sweep in range(ITERS):
        padded = jnp.concatenate([weights, jnp.zeros((BAND, TILE), jnp.float32)], axis=0)

        def band_block(block):
            tiles = band_tiles[block] * shape_mask
            column_bias = lax.dynamic_slice_in_dim(padded, block, BAND + 1, 0)
            here = padded[block]
            row_terms = here * jnp.einsum("kij,kj->i", tiles, column_bias, precision=HIGH)
            row_terms = row_terms - here * here * jnp.diagonal(tiles[0])
            col_terms = column_bias * jnp.einsum("kij,i->kj", tiles, here, precision=HIGH)
            return row_terms, col_terms

        row_terms, col_terms = lax.map(band_block, jnp.arange(NB, dtype=jnp.int32))
        totals = row_terms
        for offset in range(BAND + 1):
            totals = totals.at[offset:].add(col_terms[:NB - offset, offset])

        def trans_one(which):
            tile = trans_tiles[which]
            row_bias = weights[trans_rows[which]] * active[which]
            col_bias = weights[trans_cols[which]] * active[which]
            return (row_bias * jnp.dot(tile, col_bias, precision=HIGH),
                    col_bias * jnp.dot(row_bias, tile, precision=HIGH))

        trans_row, trans_col = lax.map(trans_one, jnp.arange(trans_tiles.shape[0], dtype=jnp.int32))
        totals = totals + jax.ops.segment_sum(trans_row, trans_rows, NB)
        totals = totals + jax.ops.segment_sum(trans_col, trans_cols, NB)
        average = jnp.sum(totals * unmasked) / jnp.sum(unmasked)
        coverage = totals
        weights = unmasked * weights / jnp.where(unmasked > 0, totals / average, 1.0)
    return weights.reshape(-1), coverage.reshape(-1)
```

```python
import functools

import jax
import jax.numpy as jnp
from jax import lax
from jax.experimental import pallas as pl
from jax.experimental.pallas import tpu as pltpu
from jax.sharding import PartitionSpec as P

F32 = jnp.float32
I32 = jnp.int32
VMEM = pl.BlockSpec(memory_space=pltpu.VMEM)
SMEM = pl.BlockSpec(memory_space=pltpu.SMEM)
ROWS = 32
PARAMS = pltpu.CompilerParams(vmem_limit_bytes=32 * 1024 * 1024)


def rows_iota(shape):
    return lax.broadcasted_iota(I32, shape, 0)


def lanes_iota(shape):
    return lax.broadcasted_iota(I32, shape, 1)


def spread_blocks(flat):
    n = flat.shape[0] // 2
    halves = flat.reshape(n, 2, 128)
    return jnp.concatenate([halves[:, 0], halves[:, 1]], axis=1)


def columns_of(block_rows):
    width = block_rows.shape[1]
    padded = jnp.concatenate([block_rows, jnp.zeros((120, width), F32)], axis=0)
    return jnp.transpose(padded)


def pick_lane(ref, start, lane):
    chunk = ref[pl.ds(start, ROWS), :]
    hit = lanes_iota(chunk.shape) == lane
    return jnp.sum(jnp.where(hit, chunk, 0.0), axis=1, keepdims=True)


def fold(chunk):
    total = chunk[0:8]
    for at in range(8, chunk.shape[0], 8):
        total = total + chunk[at : at + 8]
    return total


def request_kernel(masked_ref, cols_ref, count_ref, code_ref, own_ref, ahead_ref, *, blk_g):
    groups, lanes = code_ref.shape
    row = rows_iota((groups, lanes))
    code = jnp.zeros((groups, lanes), I32)
    for t in range(cols_ref.shape[0]):
        target = cols_ref[t] // blk_g
        wanted = cols_ref[t] - target * blk_g + 1
        used = t < count_ref[0]
        code = jnp.where((row == target) & used, wanted, code)
    code_ref[...] = code
    for c in range(blk_g):
        for h in range(2):
            piece = 1.0 - masked_ref[pl.ds(2 * c + h, 1), :].astype(F32)
            own_ref[pl.ds(c, 1), pl.ds(128 * h, 128)] = piece
            if c < ahead_ref.shape[0]:
                ahead_ref[pl.ds(c, 1), pl.ds(128 * h, 128)] = piece


def band_columns(band_ref, cols_scr, out_scr, anchor):
    blk_dev, spans, width, _ = band_ref.shape
    for q in range(blk_dev):
        def step(s, sums, q=q):
            start = pl.multiple_of(s * ROWS, ROWS)
            here = pick_lane(cols_scr, start, anchor + q)
            out = []
            for k in range(spans):
                chunk = band_ref[q, k, pl.ds(start, ROWS), :]
                if k == 0:
                    above = rows_iota(chunk.shape) + start < lanes_iota(chunk.shape)
                    chunk = jnp.where(above, chunk, 0.0)
                out.append(sums[k] + fold(chunk * here))
            return tuple(out)

        sums = lax.fori_loop(
            0, width // ROWS, step, tuple(jnp.zeros((8, width), F32) for _ in range(spans))
        )
        for k in range(spans):
            out_scr[pl.ds(anchor + q + k, 1), :] += jnp.sum(sums[k], axis=0, keepdims=True)


def band_rows(band_ref, ext_scr, racc_scr, anchor):
    blk_dev, spans, width, _ = band_ref.shape
    for q in range(blk_dev):
        biases = [ext_scr[pl.ds(anchor + q + k, 1), :] for k in range(spans)]

        def step(s, carry, q=q, biases=biases):
            start = pl.multiple_of(s * ROWS, ROWS)
            total = jnp.zeros((ROWS, width), F32)
            for k in range(spans):
                chunk = band_ref[q, k, pl.ds(start, ROWS), :]
                if k == 0:
                    upper = rows_iota(chunk.shape) + start <= lanes_iota(chunk.shape)
                    chunk = jnp.where(upper, chunk, 0.0)
                total = total + chunk * biases[k]
            summed = jnp.sum(total, axis=1, keepdims=True)
            hit = lanes_iota((ROWS, 128)) == anchor + q
            racc_scr[pl.ds(start, ROWS), :] += jnp.where(hit, summed, 0.0)
            return carry

        lax.fori_loop(0, width // ROWS, step, 0)


def trans_columns(trans_ref, rows_ref, count_ref, cols_scr, base, y_ref):
    tiles, width, _ = trans_ref.shape
    y_ref[...] = jnp.zeros(y_ref.shape, F32)

    def one(t, carry):
        lane = jnp.where(t < count_ref[0], rows_ref[t] - base, 127)

        def step(s, total):
            start = pl.multiple_of(s * ROWS, ROWS)
            here = pick_lane(cols_scr, start, lane)
            return total + fold(trans_ref[t, pl.ds(start, ROWS), :] * here)

        total = lax.fori_loop(0, width // ROWS, step, jnp.zeros((8, width), F32), unroll=True)
        y_ref[pl.ds(t, 1), :] = jnp.sum(total, axis=0, keepdims=True)
        return carry

    lax.fori_loop(0, tiles, one, 0)


def trans_rows_sum(trans_ref, rows_ref, cols_ref, count_ref, got_ref, racc_scr, base, blk_g):
    tiles, width, _ = trans_ref.shape

    def one(t, carry):
        used = t < count_ref[0]
        lane = jnp.where(used, rows_ref[t] - base, 127)
        source = jnp.where(used, cols_ref[t] // blk_g, 0)
        bias = got_ref[pl.ds(source, 1), :]

        def step(s, c):
            start = pl.multiple_of(s * ROWS, ROWS)
            summed = jnp.sum(trans_ref[t, pl.ds(start, ROWS), :] * bias, axis=1, keepdims=True)
            hit = lanes_iota((ROWS, 128)) == lane
            racc_scr[pl.ds(start, ROWS), :] += jnp.where(hit, summed, 0.0)
            return c

        lax.fori_loop(0, width // ROWS, step, 0, unroll=True)
        return carry

    lax.fori_loop(0, tiles, one, 0)


def owner_sums(code_ref, got_ref, blk_g):
    width = got_ref.shape[1]
    out = []
    for c in range(blk_g):
        total = jnp.zeros((8, width), F32)
        for at in range(0, code_ref.shape[0], 8):
            hit = code_ref[at : at + 8, :] == c + 1
            hit = jnp.concatenate([hit] * (width // 128), axis=1)
            total = total + jnp.where(hit, got_ref[at : at + 8, :], 0.0)
        out.append(jnp.sum(total, axis=0, keepdims=True))
    return jnp.concatenate(out, axis=0)


def pack(code_ref, own, y_ref, cols_ref, count_ref, send_ref, blk_g):
    groups, width = send_ref.shape
    for at in range(0, groups, 8):
        code = code_ref[at : at + 8, :]
        for h in range(0, width, 128):
            piece = jnp.zeros((8, 128), F32)
            for c in range(blk_g):
                piece = jnp.where(code == c + 1, own[c : c + 1, h : h + 128], piece)
            send_ref[at : at + 8, h : h + 128] = piece
    for t in range(cols_ref.shape[0]):
        @pl.when(t < count_ref[0])
        def _(t=t):
            send_ref[pl.ds(cols_ref[t] // blk_g, 1), :] = y_ref[pl.ds(t, 1), :]


def first_kernel(own_ref, ahead_ref, band_ref, trans_ref, rows_ref, count_ref,
                 y_ref, part_ref, spill_ref, ext_scr, cols_scr, racc_scr, csum_scr):
    blk_g = own_ref.shape[0]
    reach = ahead_ref.shape[0]
    anchor = lax.axis_index("rep") * band_ref.shape[0]
    base = lax.axis_index("genome") * blk_g
    own = own_ref[...]
    ext_scr[0:blk_g, :] = own
    ext_scr[blk_g : blk_g + reach, :] = ahead_ref[...]
    cols_scr[...] = columns_of(own)
    racc_scr[...] = jnp.zeros(racc_scr.shape, F32)
    csum_scr[...] = jnp.zeros(csum_scr.shape, F32)
    trans_columns(trans_ref, rows_ref, count_ref, cols_scr, base, y_ref)
    band_columns(band_ref, cols_scr, csum_scr, anchor)
    band_rows(band_ref, ext_scr, racc_scr, anchor)
    part_ref[...] = csum_scr[0:blk_g, :] + jnp.transpose(racc_scr[...])[0:blk_g, :]
    spill_ref[...] = csum_scr[blk_g : blk_g + reach, :]


def pack_kernel(code_ref, own_ref, y_ref, cols_ref, count_ref, send_ref):
    pack(code_ref, own_ref[...], y_ref, cols_ref, count_ref, send_ref, own_ref.shape[0])


def gather_kernel(code_ref, got_ref, part_ref, back_ref, trans_ref, rows_ref, cols_ref, count_ref,
                  share_ref, racc_scr):
    blk_g, width = part_ref.shape
    reach = back_ref.shape[0]
    base = lax.axis_index("genome") * blk_g
    racc_scr[...] = jnp.zeros(racc_scr.shape, F32)
    trans_rows_sum(trans_ref, rows_ref, cols_ref, count_ref, got_ref, racc_scr, base, blk_g)
    total = part_ref[...] + jnp.transpose(racc_scr[...])[0:blk_g, :]
    total = total + owner_sums(code_ref, got_ref, blk_g)
    total = total + jnp.concatenate([back_ref[...], jnp.zeros((blk_g - reach, width), F32)], axis=0)
    for s in range(share_ref.shape[0]):
        share_ref[s] = total


def second_kernel(shares_ref, own_ref, code_ref, band_ref, trans_ref, rows_ref, cols_ref, count_ref,
                  bias_ref, send_ref, ahead_ref, spill_ref, part_ref, first_ref,
                  cols_scr, csum_scr, y_scr):
    blk_g = own_ref.shape[0]
    reach = ahead_ref.shape[0]
    anchor = lax.axis_index("rep") * band_ref.shape[0]
    base = lax.axis_index("genome") * blk_g
    own = own_ref[...]
    total = shares_ref[0]
    for s in range(1, shares_ref.shape[0]):
        total = total + shares_ref[s]
    kept = own > 0.0
    bias = jnp.where(kept, 1.0 / jnp.where(kept, total, 1.0), 0.0)
    bias_ref[...] = bias
    ahead_ref[...] = bias[0:reach]
    first_ref[...] = jnp.where(kept, total, 0.0)
    cols_scr[...] = columns_of(bias)
    csum_scr[...] = jnp.zeros(csum_scr.shape, F32)
    trans_columns(trans_ref, rows_ref, count_ref, cols_scr, base, y_scr)
    band_columns(band_ref, cols_scr, csum_scr, anchor)
    part_ref[...] = csum_scr[0:blk_g, :]
    spill_ref[...] = csum_scr[blk_g : blk_g + reach, :]
    pack(code_ref, bias, y_scr, cols_ref, count_ref, send_ref, blk_g)


def third_kernel(code_ref, got_ref, part_ref, back_ref, bias_ref, ahead_ref, band_ref, trans_ref,
                 rows_ref, cols_ref, count_ref, share_ref, ext_scr, racc_scr):
    blk_g, width = part_ref.shape
    reach = back_ref.shape[0]
    anchor = lax.axis_index("rep") * band_ref.shape[0]
    base = lax.axis_index("genome") * blk_g
    ext_scr[0:blk_g, :] = bias_ref[...]
    ext_scr[blk_g : blk_g + reach, :] = ahead_ref[...]
    racc_scr[...] = jnp.zeros(racc_scr.shape, F32)
    band_rows(band_ref, ext_scr, racc_scr, anchor)
    trans_rows_sum(trans_ref, rows_ref, cols_ref, count_ref, got_ref, racc_scr, base, blk_g)
    total = part_ref[...] + jnp.transpose(racc_scr[...])[0:blk_g, :]
    total = total + owner_sums(code_ref, got_ref, blk_g)
    total = total + jnp.concatenate([back_ref[...], jnp.zeros((blk_g - reach, width), F32)], axis=0)
    for s in range(share_ref.shape[0]):
        share_ref[s] = total


def whole_sum(block):
    return jnp.sum(jnp.sum(block, axis=0, keepdims=True), axis=1, keepdims=True)


def stats_kernel(shares_ref, own_ref, bias_ref, first_ref, second_ref, stats_ref):
    total = shares_ref[0]
    for s in range(1, shares_ref.shape[0]):
        total = total + shares_ref[s]
    second_ref[...] = total
    count = whole_sum(own_ref[...])
    sum_one = whole_sum(first_ref[...])
    scale = sum_one / jnp.maximum(count, 1.0)
    scale = jnp.where(scale == 0.0, 1.0, scale)
    sum_two = whole_sum((bias_ref[...] * scale) * (total * scale))
    lane = lanes_iota(stats_ref.shape)
    stats = jnp.where(lane == 0, sum_one, 0.0)
    stats = jnp.where(lane == 1, sum_two, stats)
    stats = jnp.where(lane == 2, scale, stats)
    stats_ref[...] = jnp.where(lane == 3, count, stats)


def final_kernel(stats_ref, own_ref, bias_ref, second_ref, weights_ref, coverage_ref):
    stats = stats_ref[...]
    lane = lanes_iota(stats.shape)

    def lane_of(at):
        return jnp.sum(jnp.where(lane == at, stats, 0.0), axis=1, keepdims=True)

    count = jnp.sum(lane_of(3), axis=0, keepdims=True)
    average_one = jnp.sum(lane_of(0), axis=0, keepdims=True) / count
    ratio = average_one / lane_of(2)
    average_two = jnp.sum(lane_of(1) * ratio * ratio, axis=0, keepdims=True) / count
    own = own_ref[...]
    kept = own > 0.0
    total = second_ref[...] * average_one
    coverage = (bias_ref[...] * average_one) * total
    weights = jnp.where(kept, average_two / jnp.where(kept, total, 1.0), 0.0)
    for c in range(own.shape[0]):
        for h in range(2):
            weights_ref[pl.ds(2 * c + h, 1), :] = weights[c : c + 1, 128 * h : 128 * h + 128]
            coverage_ref[pl.ds(2 * c + h, 1), :] = coverage[c : c + 1, 128 * h : 128 * h + 128]


def call(kernel, outs, specs, scratch=()):
    return pl.pallas_call(
        kernel,
        out_shape=[jax.ShapeDtypeStruct(s, d) for s, d in outs],
        in_specs=list(specs),
        out_specs=[VMEM] * len(outs),
        scratch_shapes=[pltpu.VMEM(s, F32) for s in scratch],
        compiler_params=PARAMS,
    )


def shifted(block, axis, distance):
    devices = range(lax.axis_size(axis))
    route = [(i - distance, i) for i in devices if i - distance in devices]
    return lax.ppermute(block, axis, route)


def exchange(block, axis):
    return lax.all_to_all(block, axis, 0, 0, tiled=True)


def shards(band_tiles, trans_tiles, trans_rows, trans_cols, trans_count, masked):
    blk_dev, spans, width, _ = band_tiles.shape
    reach = spans - 1
    replicas = lax.axis_size("rep")
    groups = lax.axis_size("genome")
    blk_g = blk_dev * replicas
    halves = masked.reshape(2 * blk_g, 128)
    own_shape = (blk_g, width)
    reach_shape = (reach, width)
    code, own, ahead = call(
        functools.partial(request_kernel, blk_g=blk_g),
        [((groups, 128), I32), (own_shape, F32), (reach_shape, F32)],
        [VMEM, SMEM, SMEM],
    )(halves, trans_cols, trans_count)
    forward = shifted(ahead, "genome", -1)
    code = exchange(code, "genome")
    y, part, spill = call(
        first_kernel,
        [((8, width), F32), (own_shape, F32), (reach_shape, F32)],
        [VMEM] * 4 + [SMEM] * 2,
        [(16, width), (width, 128), (width, 128), (16, width)],
    )(own, forward, band_tiles, trans_tiles, trans_rows, trans_count)
    back = shifted(spill, "genome", 1)
    (send,) = call(
        pack_kernel, [((groups, width), F32)], [VMEM] * 3 + [SMEM] * 2
    )(code, own, y, trans_cols, trans_count)
    got = exchange(send, "genome")
    (share,) = call(
        gather_kernel,
        [((replicas,) + own_shape, F32)],
        [VMEM] * 5 + [SMEM] * 3,
        [(width, 128)],
    )(code, got, part, back, trans_tiles, trans_rows, trans_cols, trans_count)
    shares = exchange(share, "rep")
    bias, send, ahead, spill, part, first = call(
        second_kernel,
        [(own_shape, F32), ((groups, width), F32), (reach_shape, F32), (reach_shape, F32),
         (own_shape, F32), (own_shape, F32)],
        [VMEM] * 5 + [SMEM] * 3,
        [(width, 128), (16, width), (8, width)],
    )(shares, own, code, band_tiles, trans_tiles, trans_rows, trans_cols, trans_count)
    forward = shifted(ahead, "genome", -1)
    back = shifted(spill, "genome", 1)
    got = exchange(send, "genome")
    (share,) = call(
        third_kernel,
        [((replicas,) + own_shape, F32)],
        [VMEM] * 8 + [SMEM] * 3,
        [(16, width), (width, 128)],
    )(code, got, part, back, bias, forward, band_tiles, trans_tiles, trans_rows, trans_cols,
      trans_count)
    shares = exchange(share, "rep")
    second, stats = call(
        stats_kernel, [(own_shape, F32), ((groups, 128), F32)], [VMEM] * 4
    )(shares, own, bias, first)
    stats = exchange(stats, "genome")
    weights, coverage = call(
        final_kernel, [((2 * blk_g, 128), F32)] * 2, [VMEM] * 4
    )(stats, own, bias, second)
    return (weights.reshape(-1), coverage.reshape(-1))


def solution(mesh):
    in_specs = (
        P(("genome", "rep"), None, None, None),
        P(("genome", "rep"), None, None),
        P(("genome", "rep")),
        P(("genome", "rep")),
        P(("genome", "rep")),
        P("genome"),
    )
    out_specs = (P("genome"), P("genome"))
    return jax.shard_map(shards, mesh=mesh, in_specs=in_specs, out_specs=out_specs, check_vma=False)
```

```python
import functools

import jax
import jax.numpy as jnp
from jax import lax
from jax.experimental import pallas as pl
from jax.experimental.pallas import tpu as pltpu
from jax.sharding import Mesh, PartitionSpec as P

F32 = jnp.float32
I32 = jnp.int32
LANES = 128
CHUNK = 32
VMEM = pl.BlockSpec(memory_space=pltpu.VMEM)
SMEM = pl.BlockSpec(memory_space=pltpu.SMEM)
HBM = pl.BlockSpec(memory_space=pltpu.HBM)


def rows_iota(shape):
    return lax.broadcasted_iota(I32, shape, 0)


def lanes_iota(shape):
    return lax.broadcasted_iota(I32, shape, 1)


def columns_of(block_rows):
    n, width = block_rows.shape
    padded = jnp.concatenate([block_rows, jnp.zeros((LANES - n, width), F32)], axis=0)
    return jnp.transpose(padded)


def pick_lane(ref, start, lane):
    chunk = ref[start : start + CHUNK, :]
    return jnp.sum(jnp.where(lanes_iota(chunk.shape) == lane, chunk, 0.0), axis=1, keepdims=True)


def fold(chunk):
    total = chunk[0:8]
    for at in range(8, chunk.shape[0], 8):
        total = total + chunk[at : at + 8]
    return total


def put_lane(ref, start, lane, column):
    hit = lanes_iota((CHUNK, LANES)) == lane
    ref[start : start + CHUNK, :] += jnp.where(hit, column, 0.0)


def band_columns(band_ref, cols_scr, sums_scr, anchor, ready):
    blk_dev, spans, width, _ = band_ref.shape
    sums_scr[...] = jnp.zeros(sums_scr.shape, F32)

    def one(q, carry):
        ready(q)
        sums = [jnp.zeros((8, width), F32) for _ in range(spans)]
        for start in range(0, width, CHUNK):
            here = pick_lane(cols_scr, start, anchor + q)
            for k in range(spans):
                chunk = band_ref[q, k, start : start + CHUNK, :]
                if k == 0:
                    above = rows_iota(chunk.shape) + start < lanes_iota(chunk.shape)
                    chunk = jnp.where(above, chunk, 0.0)
                sums[k] = sums[k] + fold(chunk * here)
        for k in range(spans):
            sums_scr[pl.ds(anchor + q + k, 1), :] += jnp.sum(sums[k], axis=0, keepdims=True)
        return carry

    lax.fori_loop(0, blk_dev, one, 0)


def band_rows(band_ref, ext_scr, racc_scr, anchor):
    blk_dev, spans, width, _ = band_ref.shape

    def one(q, carry):
        biases = [ext_scr[pl.ds(anchor + q + k, 1), :] for k in range(spans)]
        for start in range(0, width, CHUNK):
            total = jnp.zeros((CHUNK, width), F32)
            for k in range(spans):
                chunk = band_ref[q, k, start : start + CHUNK, :]
                if k == 0:
                    upper = rows_iota(chunk.shape) + start <= lanes_iota(chunk.shape)
                    chunk = jnp.where(upper, chunk, 0.0)
                total = total + chunk * biases[k]
            put_lane(racc_scr, start, anchor + q, jnp.sum(total, axis=1, keepdims=True))
        return carry

    lax.fori_loop(0, blk_dev, one, 0)


def trans_columns(trans_ref, info_ref, cols_scr, emit, ready):
    tiles, width, _ = trans_ref.shape

    def one(t, carry):
        ready(t)
        total = jnp.zeros((8, width), F32)
        for start in range(0, width, CHUNK):
            here = pick_lane(cols_scr, start, info_ref[8 + t])
            total = total + fold(trans_ref[t, start : start + CHUNK, :] * here)
        emit(t, jnp.sum(total, axis=0, keepdims=True))
        return carry

    lax.fori_loop(0, tiles, one, 0)


def trans_rows(trans_ref, info_ref, bias_of, racc_scr):
    tiles, width, _ = trans_ref.shape

    def one(t, carry):
        near, far = bias_of(t)
        for start in range(0, width, CHUNK):
            chunk = trans_ref[t, start : start + CHUNK, :]
            total = chunk[:, :LANES] * near + chunk[:, LANES:] * far
            put_lane(racc_scr, start, info_ref[8 + t], jnp.sum(total, axis=1, keepdims=True))
        return carry

    lax.fori_loop(0, tiles, one, 0)


def add_sums(code_of, half_of, steps, blk_g):
    out = [[jnp.zeros((8, LANES), F32) for _ in range(2)] for _ in range(blk_g)]
    for step in steps:
        code = code_of(step)
        for h in range(2):
            piece = half_of(step, h)
            for c in range(blk_g):
                out[c][h] = out[c][h] + jnp.where(code == c + 1.0, piece, 0.0)
    sums = [[jnp.sum(half, axis=0, keepdims=True) for half in pair] for pair in out]
    return jnp.concatenate([jnp.concatenate(pair, axis=1) for pair in sums], axis=0)


def nothing(_):
    pass


def fill_send(bias, info_ref, band_ref, trans_ref, send_ref, part_ref, scratch, band_ready=nothing,
              trans_ready=nothing):
    cols_scr, sums_scr, flat_scr, spill_scr = scratch
    blk_g = bias.shape[0]
    blk_dev, spans = band_ref.shape[:2]
    slot = 2 * blk_g
    half = slot // 2
    reach = spans - 1
    chip, core = lax.axis_index("chip"), lax.axis_index("core")
    here = 2 * chip + core
    for h in range(2):
        flat_scr[pl.ds(h, blk_g, stride=2), :] = bias[:, LANES * h : LANES * h + LANES]
    cols_scr[...] = columns_of(bias)
    flat = flat_scr[...]
    for at in range(send_ref.shape[0] // slot):
        send_ref[slot * at : slot * at + slot, :] = jnp.where(at < chip, flat, 0.0)

    def emit(t, sums):
        base = slot * (info_ref[t] // 2)
        odd = info_ref[t] % 2
        code = jnp.where(info_ref[t] == here, 0, info_ref[16 + t] + 1).astype(F32)
        for h in range(2):
            send_ref[pl.ds(base + 2 * odd + h, 1), :] = sums[:, LANES * h : LANES * h + LANES]
        send_ref[pl.ds(base + 4 + odd, 1), :] = jnp.full((1, LANES), code, F32)

    trans_columns(trans_ref, info_ref, cols_scr, emit, trans_ready)
    anchor = lax.axis_index("rep") * blk_dev
    band_columns(band_ref, cols_scr, sums_scr, anchor, band_ready)
    part_ref[...] = sums_scr[0:blk_g, :]
    for h in range(2):
        part = sums_scr[blk_g : blk_g + reach, LANES * h : LANES * h + LANES]
        spill_scr[pl.ds(h, reach, stride=2), :] = part
    spill = spill_scr[...]
    mine = pl.multiple_of(slot * chip, slot)
    send_ref[pl.ds(mine, half), :] = flat[0:half]
    send_ref[pl.ds(mine + half, half), :] = spill

    @pl.when((core == 1) & (chip < lax.axis_size("chip") - 1))
    def _():
        send_ref[pl.ds(mine + slot + half, half), :] = spill


def first_kernel(masked_ref, cols_ref, rows_ref, count_ref, band_in, trans_in, own_ref, info_ref,
                 send_ref, part_ref, band_ref, trans_ref, sems, flat_scr, *scratch):
    blk_g = own_ref.shape[0]
    blk_dev, tiles = band_ref.shape[0], trans_ref.shape[0]

    def trans_copy(t):
        return pltpu.make_async_copy(trans_in.at[t], trans_ref.at[t], sems.at[t])

    def band_copy(q):
        return pltpu.make_async_copy(band_in.at[q], band_ref.at[q], sems.at[tiles + q])

    for t in range(tiles):
        trans_copy(t).start()
    for q in range(blk_dev):
        band_copy(q).start()
    here = 2 * lax.axis_index("chip") + lax.axis_index("core")
    for t in range(tiles):
        used = t < count_ref[0]
        target = cols_ref[t] // blk_g
        info_ref[t] = jnp.where(used, target, here)
        info_ref[8 + t] = jnp.where(used, rows_ref[t] - here * blk_g, LANES - 1)
        info_ref[16 + t] = cols_ref[t] - target * blk_g
    flat_scr[...] = 1.0 - masked_ref[...].astype(F32)
    own = jnp.concatenate([flat_scr[pl.ds(h, blk_g, stride=2), :] for h in range(2)], axis=1)
    own_ref[...] = own
    fill_send(own, info_ref, band_ref, trans_ref, send_ref, part_ref, scratch,
              lambda q: band_copy(q).wait(), lambda t: trans_copy(t).wait())


def spread(value, scr):
    scr[...] = value
    n = value.shape[0] // 2
    return jnp.concatenate([scr[pl.ds(h, n, stride=2), :] for h in range(2)], axis=1)


def fill_shares(share_ref, total):
    for s in range(share_ref.shape[0]):
        share_ref[s] = total


def meet_kernel(own_ref, part_ref, got_ref, mate_ref, info_ref, band_ref, trans_ref,
                share_ref, ext_scr, racc_scr, near_scr):
    blk_g, width = own_ref.shape
    blk_dev, spans = band_ref.shape[:2]
    reach = spans - 1
    slot = 2 * blk_g
    half = slot // 2
    chips = got_ref.shape[0] // slot
    chip, core = lax.axis_index("chip"), lax.axis_index("core")
    anchor = lax.axis_index("rep") * blk_dev
    first = core == 0
    at = pl.multiple_of(slot * jnp.minimum(chip + core, chips - 1), slot)
    ahead = jnp.where(chip + core < chips, mate_ref[pl.ds(at, half), :], 0.0)
    at = pl.multiple_of(slot * jnp.maximum(chip + core - 1, 0), slot)
    back = jnp.where(chip + core > 0, mate_ref[pl.ds(at + half, half), :], 0.0)
    ext_scr[0:blk_g, :] = own_ref[...]
    ext_scr[blk_g : blk_g + reach, :] = spread(ahead, near_scr)
    racc_scr[...] = jnp.zeros(racc_scr.shape, F32)
    band_rows(band_ref, ext_scr, racc_scr, anchor)

    def bias_of(t):
        source = info_ref[t]
        row = slot * (source // 2) + 2 * info_ref[16 + t]
        same = source % 2 == core
        return [
            jnp.where(same, got_ref[pl.ds(row + h, 1), :], mate_ref[pl.ds(row + h, 1), :])
            for h in range(2)
        ]

    trans_rows(trans_ref, info_ref, bias_of, racc_scr)

    def pick(ref, step, row):
        even, odd = row
        base = step * 8 * slot
        return jnp.where(
            first,
            ref[pl.ds(base + even, 8, stride=slot), :],
            ref[pl.ds(base + odd, 8, stride=slot), :],
        )

    steps = [(i, step) for i in range(2) for step in range(chips // 8)]
    refs = (got_ref, mate_ref)

    def code_of(which):
        i, step = which
        code = pick(refs[i], step, (4, 5))
        return jnp.where(rows_iota(code.shape) + 8 * step < chip, code, 0.0)

    sums = add_sums(code_of, lambda w, h: pick(refs[w[0]], w[1], (h, 2 + h)), steps, blk_g)
    total = part_ref[...] + jnp.transpose(racc_scr[...])[0:blk_g, :] + sums
    total = total + jnp.concatenate(
        [spread(back, near_scr), jnp.zeros((blk_g - reach, width), F32)], axis=0
    )
    fill_shares(share_ref, total)


def total_of(shares_ref):
    total = shares_ref[0]
    for s in range(1, shares_ref.shape[0]):
        total = total + shares_ref[s]
    return total


def second_kernel(shares_ref, own_ref, info_ref, band_ref, trans_ref, bias_ref, first_ref, send_ref,
                  part_ref, *scratch):
    kept = own_ref[...] > 0.0
    total = total_of(shares_ref)
    bias = jnp.where(kept, 1.0 / jnp.where(kept, total, 1.0), 0.0)
    bias_ref[...] = bias
    first_ref[...] = jnp.where(kept, total, 0.0)
    fill_send(bias, info_ref, band_ref, trans_ref, send_ref, part_ref, scratch)


def whole_sum(block):
    return jnp.sum(jnp.sum(block, axis=0, keepdims=True), axis=1, keepdims=True)


def stats_kernel(shares_ref, own_ref, bias_ref, first_ref, second_ref, stats_ref):
    total = total_of(shares_ref)
    second_ref[...] = total
    count = whole_sum(own_ref[...])
    sum_one = whole_sum(first_ref[...])
    scale = sum_one / jnp.maximum(count, 1.0)
    scale = jnp.where(scale == 0.0, 1.0, scale)
    sum_two = whole_sum((bias_ref[...] * scale) * (total * scale))
    lane = lanes_iota(stats_ref.shape)
    stats = jnp.where(lane == 0, sum_one, 0.0)
    stats = jnp.where(lane == 1, sum_two, stats)
    stats = jnp.where(lane == 2, scale, stats)
    stats_ref[...] = jnp.where(lane == 3, count, stats)


def final_kernel(stats_ref, own_ref, bias_ref, second_ref, weights_ref, coverage_ref):
    stats = stats_ref[...]
    lane = lanes_iota(stats.shape)

    def lane_of(at):
        return jnp.sum(jnp.where(lane == at, stats, 0.0), axis=1, keepdims=True)

    count = jnp.sum(lane_of(3), axis=0, keepdims=True)
    average_one = jnp.sum(lane_of(0), axis=0, keepdims=True) / count
    ratio = average_one / lane_of(2)
    average_two = jnp.sum(lane_of(1) * ratio * ratio, axis=0, keepdims=True) / count
    own = own_ref[...]
    blk_g = own.shape[0]
    kept = own > 0.0
    total = second_ref[...] * average_one
    coverage = (bias_ref[...] * average_one) * total
    weights = jnp.where(kept, average_two / jnp.where(kept, total, 1.0), 0.0)
    for h in range(2):
        part = slice(LANES * h, LANES * h + LANES)
        weights_ref[pl.ds(h, blk_g, stride=2), :] = weights[:, part]
        coverage_ref[pl.ds(h, blk_g, stride=2), :] = coverage[:, part]


def call(kernel, ins, outs, scratch=(), cost=None, limit=16):
    return pl.pallas_call(
        kernel,
        in_specs=list(ins),
        out_shape=[jax.ShapeDtypeStruct(s, d) for s, d, _ in outs],
        out_specs=[spec for _, _, spec in outs],
        scratch_shapes=list(scratch),
        compiler_params=pltpu.CompilerParams(vmem_limit_bytes=limit * 1024 * 1024),
        cost_estimate=cost and pl.CostEstimate(flops=cost, bytes_accessed=cost, transcendentals=0),
    )


def floats(*shape):
    return (shape, F32, VMEM)


def exchange(block, axis):
    return lax.all_to_all(block, axis, 0, 0, tiled=True)


def swap_cores(block):
    return lax.ppermute(block, "core", [(0, 1), (1, 0)])


def shards(band, trans, rows_at, cols_at, trans_count, masked):
    blk_dev, spans, width, _ = band.shape
    tiles = trans.shape[0]
    replicas = lax.axis_size("rep")
    chips = lax.axis_size("chip")
    blk_g = blk_dev * replicas
    own_like = floats(blk_g, width)
    send_like = floats(chips * 2 * blk_g, LANES)
    cols_scr = pltpu.VMEM((width, LANES), F32)
    wide_scr = pltpu.VMEM((16, width), F32)
    flat_scr = pltpu.VMEM((2 * blk_g, LANES), F32)
    half_scr = pltpu.VMEM((2 * spans - 2, LANES), F32)
    fill_scr = [cols_scr, wide_scr, flat_scr, half_scr]
    own, info, send, part = call(
        first_kernel,
        [VMEM, SMEM, SMEM, SMEM, HBM, HBM],
        [own_like, ((24,), I32, SMEM), send_like, own_like],
        [pltpu.VMEM(band.shape, F32), pltpu.VMEM(trans.shape, F32),
         pltpu.SemaphoreType.DMA((tiles + blk_dev,)), flat_scr] + fill_scr,
        limit=52,
    )(masked.reshape(2 * blk_g, LANES), cols_at, rows_at, trans_count, band, trans)
    bias = own
    for sweep in range(2):
        got = exchange(send, "chip")
        mate = swap_cores(got)
        (share,) = call(
            meet_kernel,
            [VMEM, VMEM, VMEM, VMEM, SMEM, VMEM, VMEM],
            [floats(replicas, blk_g, width)],
            [wide_scr, cols_scr, half_scr],
        )(bias, part, got, mate, info, band, trans)
        shares = exchange(share, "rep")
        if not sweep:
            bias, first, send, part = call(
                second_kernel,
                [VMEM, VMEM, SMEM, VMEM, VMEM],
                [own_like, own_like, send_like, own_like],
                fill_scr,
            )(shares, own, info, band, trans)
    second, stats = call(
        stats_kernel, [VMEM] * 4, [own_like, floats(2 * chips, LANES)]
    )(shares, own, bias, first)
    stats = exchange(stats, GENOME)
    weights, coverage = call(
        final_kernel, [VMEM] * 4, [floats(2 * blk_g, LANES)] * 2
    )(stats, own, bias, second)
    return (weights.reshape(-1), coverage.reshape(-1))


GENOME = ("chip", "core")


def solution(mesh):
    names = mesh.axis_names
    groups, replicas = (mesh.shape[name] for name in ("genome", "rep"))
    assert names == ("genome", "rep")
    devices = mesh.devices.reshape(groups // 2, 2, replicas)
    split = Mesh(devices, GENOME + ("rep",))
    every = P(GENOME + ("rep",))
    out_specs = (P(GENOME), P(GENOME))
    return jax.shard_map(
        shards, mesh=split, in_specs=(every,) * 5 + (P(GENOME),), out_specs=out_specs, check_vma=False
    )
```

```python
import functools

import jax
import jax.numpy as jnp
from jax import lax
from jax.experimental import pallas as pl
from jax.experimental.pallas import tpu as pltpu
from jax.sharding import Mesh, PartitionSpec as P

F32 = jnp.float32
I32 = jnp.int32
LANES = 128
CHUNK = 32
VMEM = pl.BlockSpec(memory_space=pltpu.VMEM)
SMEM = pl.BlockSpec(memory_space=pltpu.SMEM)
HBM = pl.BlockSpec(memory_space=pltpu.HBM)


def rows_iota(shape):
    return lax.broadcasted_iota(I32, shape, 0)


def lanes_iota(shape):
    return lax.broadcasted_iota(I32, shape, 1)


def columns_of(block_rows):
    n, width = block_rows.shape
    padded = jnp.concatenate([block_rows, jnp.zeros((LANES - n, width), F32)], axis=0)
    return jnp.transpose(padded)


def pick_lane(ref, start, lane):
    chunk = ref[start : start + CHUNK, :]
    return jnp.sum(jnp.where(lanes_iota(chunk.shape) == lane, chunk, 0.0), axis=1, keepdims=True)


def fold(chunk):
    total = chunk[0:8]
    for at in range(8, chunk.shape[0], 8):
        total = total + chunk[at : at + 8]
    return total


def put_lane(ref, start, lane, column):
    hit = lanes_iota((CHUNK, LANES)) == lane
    ref[start : start + CHUNK, :] += jnp.where(hit, column, 0.0)


def band_columns(band_ref, cols_scr, sums_scr, anchor, ready):
    blk_dev, spans, width, _ = band_ref.shape
    sums_scr[...] = jnp.zeros(sums_scr.shape, F32)

    def one(q, carry):
        ready(q)
        sums = [jnp.zeros((8, width), F32) for _ in range(spans)]
        for start in range(0, width, CHUNK):
            here = pick_lane(cols_scr, start, anchor + q)
            for k in range(spans):
                chunk = band_ref[q, k, start : start + CHUNK, :]
                if k == 0:
                    above = rows_iota(chunk.shape) + start < lanes_iota(chunk.shape)
                    chunk = jnp.where(above, chunk, 0.0)
                sums[k] = sums[k] + fold(chunk * here)
        for k in range(spans):
            sums_scr[pl.ds(anchor + q + k, 1), :] += jnp.sum(sums[k], axis=0, keepdims=True)
        return carry

    lax.fori_loop(0, blk_dev, one, 0)


def band_rows(band_ref, ext_scr, racc_scr, anchor):
    blk_dev, spans, width, _ = band_ref.shape

    def one(q, carry):
        biases = [ext_scr[pl.ds(anchor + q + k, 1), :] for k in range(spans)]
        for start in range(0, width, CHUNK):
            total = jnp.zeros((CHUNK, width), F32)
            for k in range(spans):
                chunk = band_ref[q, k, start : start + CHUNK, :]
                if k == 0:
                    upper = rows_iota(chunk.shape) + start <= lanes_iota(chunk.shape)
                    chunk = jnp.where(upper, chunk, 0.0)
                total = total + chunk * biases[k]
            put_lane(racc_scr, start, anchor + q, jnp.sum(total, axis=1, keepdims=True))
        return carry

    lax.fori_loop(0, blk_dev, one, 0)


def trans_columns(trans_ref, info_ref, cols_scr, emit, ready):
    tiles, width, _ = trans_ref.shape

    def one(t, carry):
        ready(t)
        total = jnp.zeros((8, width), F32)
        for start in range(0, width, CHUNK):
            here = pick_lane(cols_scr, start, info_ref[8 + t])
            total = total + fold(trans_ref[t, start : start + CHUNK, :] * here)
        emit(t, jnp.sum(total, axis=0, keepdims=True))
        return carry

    lax.fori_loop(0, tiles, one, 0)


def trans_rows(trans_ref, info_ref, bias_of, racc_scr):
    tiles, width, _ = trans_ref.shape

    def one(t, carry):
        near, far = bias_of(t)
        for start in range(0, width, CHUNK):
            chunk = trans_ref[t, start : start + CHUNK, :]
            total = chunk[:, :LANES] * near + chunk[:, LANES:] * far
            put_lane(racc_scr, start, info_ref[8 + t], jnp.sum(total, axis=1, keepdims=True))
        return carry

    lax.fori_loop(0, tiles, one, 0)


def add_sums(code_of, half_of, steps, blk_g):
    out = [[jnp.zeros((8, LANES), F32) for _ in range(2)] for _ in range(blk_g)]
    for step in steps:
        code = code_of(step)
        for h in range(2):
            piece = half_of(step, h)
            for c in range(blk_g):
                out[c][h] = out[c][h] + jnp.where(code == c + 1.0, piece, 0.0)
    sums = [[jnp.sum(half, axis=0, keepdims=True) for half in pair] for pair in out]
    return jnp.concatenate([jnp.concatenate(pair, axis=1) for pair in sums], axis=0)


def nothing(_):
    pass


def fill_send(bias, info_ref, band_ref, trans_ref, send_ref, part_ref, scratch, band_ready=nothing,
              trans_ready=nothing):
    cols_scr, sums_scr, flat_scr, spill_scr = scratch
    blk_g = bias.shape[0]
    blk_dev, spans = band_ref.shape[:2]
    slot = 2 * blk_g
    half = slot // 2
    reach = spans - 1
    chip, core = lax.axis_index("chip"), lax.axis_index("core")
    here = 2 * chip + core
    for h in range(2):
        flat_scr[pl.ds(h, blk_g, stride=2), :] = bias[:, LANES * h : LANES * h + LANES]
    cols_scr[...] = columns_of(bias)
    flat = flat_scr[...]
    for at in range(send_ref.shape[0] // slot):
        send_ref[slot * at : slot * at + slot, :] = jnp.where(at < chip, flat, 0.0)

    def emit(t, sums):
        base = slot * (info_ref[t] // 2)
        odd = info_ref[t] % 2
        code = jnp.where(info_ref[t] == here, 0, info_ref[16 + t] + 1).astype(F32)
        for h in range(2):
            send_ref[pl.ds(base + 2 * odd + h, 1), :] = sums[:, LANES * h : LANES * h + LANES]
        send_ref[pl.ds(base + 4 + odd, 1), :] = jnp.full((1, LANES), code, F32)

    trans_columns(trans_ref, info_ref, cols_scr, emit, trans_ready)
    anchor = lax.axis_index("rep") * blk_dev
    band_columns(band_ref, cols_scr, sums_scr, anchor, band_ready)
    part_ref[...] = sums_scr[0:blk_g, :]
    for h in range(2):
        part = sums_scr[blk_g : blk_g + reach, LANES * h : LANES * h + LANES]
        spill_scr[pl.ds(h, reach, stride=2), :] = part
    spill = spill_scr[...]
    mine = pl.multiple_of(slot * chip, slot)
    send_ref[pl.ds(mine, half), :] = flat[0:half]
    send_ref[pl.ds(mine + half, half), :] = spill

    @pl.when((core == 1) & (chip < lax.axis_size("chip") - 1))
    def _():
        send_ref[pl.ds(mine + slot + half, half), :] = spill


def first_kernel(masked_ref, cols_ref, rows_ref, count_ref, band_in, trans_in, own_ref, info_ref,
                 send_ref, part_ref, band_ref, trans_ref, sems, flat_scr, *scratch):
    blk_g = own_ref.shape[0]
    blk_dev, tiles = band_ref.shape[0], trans_ref.shape[0]

    def trans_copy(t):
        return pltpu.make_async_copy(trans_in.at[t], trans_ref.at[t], sems.at[t])

    def band_copy(q):
        return pltpu.make_async_copy(band_in.at[q], band_ref.at[q], sems.at[tiles + q])

    for t in range(tiles):
        trans_copy(t).start()
    for q in range(blk_dev):
        band_copy(q).start()
    here = 2 * lax.axis_index("chip") + lax.axis_index("core")
    for t in range(tiles):
        used = t < count_ref[0]
        target = cols_ref[t] // blk_g
        info_ref[t] = jnp.where(used, target, here)
        info_ref[8 + t] = jnp.where(used, rows_ref[t] - here * blk_g, LANES - 1)
        info_ref[16 + t] = cols_ref[t] - target * blk_g
    flat_scr[...] = 1.0 - masked_ref[...].astype(F32)
    own = jnp.concatenate([flat_scr[pl.ds(h, blk_g, stride=2), :] for h in range(2)], axis=1)
    own_ref[...] = own
    fill_send(own, info_ref, band_ref, trans_ref, send_ref, part_ref, scratch,
              lambda q: band_copy(q).wait(), lambda t: trans_copy(t).wait())


def spread(value, scr):
    scr[...] = value
    n = value.shape[0] // 2
    return jnp.concatenate([scr[pl.ds(h, n, stride=2), :] for h in range(2)], axis=1)


def meet_kernel(own_ref, part_ref, got_ref, mate_ref, info_ref, band_ref, trans_ref,
                share_ref, code_ref, ext_scr, racc_scr, near_scr):
    blk_g, width = own_ref.shape
    blk_dev, spans = band_ref.shape[:2]
    reach = spans - 1
    slot = 2 * blk_g
    half = slot // 2
    chips = got_ref.shape[0] // slot
    chip, core = lax.axis_index("chip"), lax.axis_index("core")
    anchor = lax.axis_index("rep") * blk_dev
    first = core == 0
    at = pl.multiple_of(slot * jnp.minimum(chip + core, chips - 1), slot)
    ahead = jnp.where(chip + core < chips, mate_ref[pl.ds(at, half), :], 0.0)
    at = pl.multiple_of(slot * jnp.maximum(chip + core - 1, 0), slot)
    back = jnp.where(chip + core > 0, mate_ref[pl.ds(at + half, half), :], 0.0)
    ext_scr[0:blk_g, :] = own_ref[...]
    ext_scr[blk_g : blk_g + reach, :] = spread(ahead, near_scr)
    racc_scr[...] = jnp.zeros(racc_scr.shape, F32)
    band_rows(band_ref, ext_scr, racc_scr, anchor)

    def bias_of(t):
        source = info_ref[t]
        row = slot * (source // 2) + 2 * info_ref[16 + t]
        same = source % 2 == core
        return [
            jnp.where(same, got_ref[pl.ds(row + h, 1), :], mate_ref[pl.ds(row + h, 1), :])
            for h in range(2)
        ]

    trans_rows(trans_ref, info_ref, bias_of, racc_scr)

    def pick(ref, step, row):
        even, odd = row
        base = step * 8 * slot
        return jnp.where(
            first,
            ref[pl.ds(base + even, 8, stride=slot), :],
            ref[pl.ds(base + odd, 8, stride=slot), :],
        )

    steps = [(i, step) for i in range(2) for step in range(chips // 8)]
    refs = (got_ref, mate_ref)

    def code_of(which):
        i, step = which
        code = pick(refs[i], step, (4, 5))
        return jnp.where(rows_iota(code.shape) + 8 * step < chip, code, 0.0)

    sums = add_sums(code_of, lambda w, h: pick(refs[w[0]], w[1], (h, 2 + h)), steps, blk_g)
    for i in range(2):
        code = got_ref[pl.ds(4 + i, chips, stride=slot), :]
        code_ref[i] = jnp.where(rows_iota(code.shape) < chip, code, 0.0)
    total = part_ref[...] + jnp.transpose(racc_scr[...])[0:blk_g, :] + sums
    total = total + jnp.concatenate(
        [spread(back, near_scr), jnp.zeros((blk_g - reach, width), F32)], axis=0
    )
    total = jnp.where(own_ref[...] > 0.0, total, jnp.inf)
    for s in range(share_ref.shape[0]):
        share_ref[s] = total


def halves(block):
    return [block[:, LANES * h : LANES * h + LANES] for h in range(2)]


def second_kernel(shares_ref, code_ref, info_ref, band_ref, trans_ref, ext_ref, first_ref, send_ref,
                  part_ref, cols_scr, sums_scr, spill_scr, ahead_scr):
    blk_g = first_ref.shape[0]
    blk_dev, spans = band_ref.shape[:2]
    reach = spans - 1
    replicas = shares_ref.shape[0] // 2
    chips = send_ref.shape[0] // STEP
    chip, core = lax.axis_index("chip"), lax.axis_index("core")
    first = core == 0
    totals, biases = [], []
    for c in range(2):
        total = shares_ref[c * replicas]
        for s in range(1, replicas):
            total = total + shares_ref[c * replicas + s]
        kept = total != jnp.inf
        totals.append(jnp.where(kept, total, 0.0))
        biases.append(jnp.where(kept, 1.0 / jnp.where(kept, total, 1.0), 0.0))
    first_ref[...] = jnp.where(first, totals[0], totals[1])
    own = jnp.where(first, biases[0], biases[1])
    ext_ref[0:blk_g, :] = own
    ext_ref[blk_g : blk_g + reach, :] = biases[1][0:reach]
    ext_ref[blk_g + reach :, :] = jnp.zeros((ext_ref.shape[0] - blk_g - reach, own.shape[1]), F32)
    cols_scr[...] = columns_of(own)
    for at in range(0, send_ref.shape[0], 8):
        send_ref[at : at + 8, :] = jnp.zeros((8, LANES), F32)
    for i in range(2):
        pieces = halves(biases[i])
        for at in range(0, chips, 8):
            code = code_ref[i, at : at + 8, :]
            for h in range(2):
                piece = jnp.zeros((8, LANES), F32)
                for c in range(blk_g):
                    piece = jnp.where(code == c + 1.0, pieces[h][c : c + 1], piece)
                send_ref[pl.ds(STEP * at + 2 - 2 * i + h, 8, stride=STEP), :] = piece

    def emit(t, sums):
        base = STEP * (info_ref[t] // 2) + 2 - 2 * (info_ref[t] % 2)
        for h in range(2):
            send_ref[pl.ds(base + h, 1), :] = halves(sums)[h]

    trans_columns(trans_ref, info_ref, cols_scr, emit, nothing)
    band_columns(band_ref, cols_scr, sums_scr, lax.axis_index("rep") * blk_dev, nothing)
    spill = sums_scr[blk_g : blk_g + reach, :]
    part_ref[0:blk_g, :] = sums_scr[0:blk_g, :]
    mate = jnp.concatenate([spill, jnp.zeros((blk_g - reach, own.shape[1]), F32)], axis=0)
    part_ref[blk_g : 2 * blk_g, :] = jnp.where(first, mate, 0.0)
    for h in range(2):
        spill_scr[pl.ds(h, reach, stride=2), :] = halves(spill)[h]
        ahead_scr[pl.ds(h, reach, stride=2), :] = halves(biases[0])[h][0:reach]

    @pl.when((core == 1) & (chip > 0))
    def _():
        for i in range(2 * reach):
            send_ref[pl.ds(STEP * (chip - 1) + 2 + i, 1), :] = ahead_scr[i : i + 1, :]

    @pl.when((core == 1) & (chip < chips - 1))
    def _():
        for i in range(2 * reach):
            send_ref[pl.ds(STEP * (chip + 1) + 2 + i, 1), :] = spill_scr[i : i + 1, :]


def third_kernel(code_ref, got_ref, ext_ref, part_ref, info_ref, band_ref, trans_ref, share_ref,
                 ext_scr, racc_scr, near_scr):
    blk_g = part_ref.shape[0] // 2
    blk_dev, spans = band_ref.shape[:2]
    reach = spans - 1
    replicas = share_ref.shape[0] // 2
    chips = got_ref.shape[0] // STEP
    chip, core = lax.axis_index("chip"), lax.axis_index("core")
    first = core == 0
    ext_scr[...] = ext_ref[...]
    racc_scr[...] = jnp.zeros(racc_scr.shape, F32)

    def edge(at, valid):
        at = jnp.clip(at, 0, chips - 1)
        for i in range(2 * reach):
            near_scr[i : i + 1, :] = got_ref[pl.ds(STEP * at + 2 + i, 1), :]
        block = jnp.concatenate([near_scr[pl.ds(h, reach, stride=2), :] for h in range(2)], axis=1)
        return jnp.where(valid, block, 0.0)

    ahead = edge(chip + 1, chip + 1 < chips)
    ext_scr[blk_g : blk_g + reach, :] = jnp.where(first, ext_ref[blk_g : blk_g + reach, :], ahead)
    back = edge(chip - 1, (core == 1) & (chip > 0))
    band_rows(band_ref, ext_scr, racc_scr, lax.axis_index("rep") * blk_dev)

    def bias_of(t):
        base = STEP * (info_ref[t] // 2) + 2 - 2 * (info_ref[t] % 2)
        return [got_ref[pl.ds(base + h, 1), :] for h in range(2)]

    trans_rows(trans_ref, info_ref, bias_of, racc_scr)
    sums = [
        add_sums(
            lambda at: code_ref[i, at : at + 8, :],
            lambda at, h: got_ref[pl.ds(STEP * at + 2 - 2 * i + h, 8, stride=STEP), :],
            range(0, chips, 8),
            blk_g,
        )
        for i in range(2)
    ]
    own = part_ref[0:blk_g, :] + jnp.transpose(racc_scr[...])[0:blk_g, :]
    own = own + jnp.where(first, sums[0], sums[1])
    mate = part_ref[blk_g : 2 * blk_g, :] + jnp.where(first, sums[1], sums[0])
    mate = mate + jnp.concatenate([back, jnp.zeros((blk_g - reach, own.shape[1]), F32)], axis=0)
    for c in range(2):
        block = jnp.where(core == c, own, mate)
        for s in range(replicas):
            share_ref[c * replicas + s] = block


def whole_sum(block):
    return jnp.sum(jnp.sum(block, axis=0, keepdims=True), axis=1, keepdims=True)


def stats_kernel(shares_ref, own_ref, ext_ref, first_ref, second_ref, stats_ref):
    bias = ext_ref[0 : own_ref.shape[0], :]
    total = shares_ref[0]
    for s in range(1, shares_ref.shape[0]):
        total = total + shares_ref[s]
    second_ref[...] = total
    count = whole_sum(own_ref[...])
    sum_one = whole_sum(first_ref[...])
    scale = sum_one / jnp.maximum(count, 1.0)
    scale = jnp.where(scale == 0.0, 1.0, scale)
    sum_two = whole_sum((bias * scale) * (total * scale))
    lane = lanes_iota(stats_ref.shape)
    stats = jnp.where(lane == 0, sum_one, 0.0)
    stats = jnp.where(lane == 1, sum_two, stats)
    stats = jnp.where(lane == 2, scale, stats)
    stats_ref[...] = jnp.where(lane == 3, count, stats)


def final_kernel(stats_ref, own_ref, ext_ref, second_ref, weights_ref, coverage_ref):
    stats = stats_ref[...]
    lane = lanes_iota(stats.shape)

    def lane_of(at):
        return jnp.sum(jnp.where(lane == at, stats, 0.0), axis=1, keepdims=True)

    count = jnp.sum(lane_of(3), axis=0, keepdims=True)
    average_one = jnp.sum(lane_of(0), axis=0, keepdims=True) / count
    ratio = average_one / lane_of(2)
    average_two = jnp.sum(lane_of(1) * ratio * ratio, axis=0, keepdims=True) / count
    own = own_ref[...]
    blk_g = own.shape[0]
    kept = own > 0.0
    total = second_ref[...] * average_one
    coverage = (ext_ref[0:blk_g, :] * average_one) * total
    weights = jnp.where(kept, average_two / jnp.where(kept, total, 1.0), 0.0)
    for h in range(2):
        part = slice(LANES * h, LANES * h + LANES)
        weights_ref[pl.ds(h, blk_g, stride=2), :] = weights[:, part]
        coverage_ref[pl.ds(h, blk_g, stride=2), :] = coverage[:, part]


def call(kernel, ins, outs, scratch=(), cost=None, limit=16):
    return pl.pallas_call(
        kernel,
        in_specs=list(ins),
        out_shape=[jax.ShapeDtypeStruct(s, d) for s, d, _ in outs],
        out_specs=[spec for _, _, spec in outs],
        scratch_shapes=list(scratch),
        compiler_params=pltpu.CompilerParams(vmem_limit_bytes=limit * 1024 * 1024),
        cost_estimate=cost and pl.CostEstimate(flops=cost, bytes_accessed=cost, transcendentals=0),
    )


def floats(*shape):
    return (shape, F32, VMEM)


def exchange(block, axis):
    return lax.all_to_all(block, axis, 0, 0, tiled=True)


def swap_cores(block):
    return lax.ppermute(block, "core", [(0, 1), (1, 0)])


def shards(band, trans, rows_at, cols_at, trans_count, masked):
    blk_dev, spans, width, _ = band.shape
    tiles = trans.shape[0]
    replicas = lax.axis_size("rep")
    chips = lax.axis_size("chip")
    blk_g = blk_dev * replicas
    own_like = floats(blk_g, width)
    send_like = floats(chips * 2 * blk_g, LANES)
    share_like = floats(2 * replicas, blk_g, width)
    cols_scr = pltpu.VMEM((width, LANES), F32)
    wide_scr = pltpu.VMEM((16, width), F32)
    flat_scr = pltpu.VMEM((2 * blk_g, LANES), F32)
    half_scr = pltpu.VMEM((2 * spans - 2, LANES), F32)
    fill_scr = [cols_scr, wide_scr, flat_scr, half_scr]
    own, info, send, part = call(
        first_kernel,
        [VMEM, SMEM, SMEM, SMEM, HBM, HBM],
        [own_like, ((24,), I32, SMEM), send_like, own_like],
        [pltpu.VMEM(band.shape, F32), pltpu.VMEM(trans.shape, F32),
         pltpu.SemaphoreType.DMA((tiles + blk_dev,)), flat_scr] + fill_scr,
        limit=52,
    )(masked.reshape(2 * blk_g, LANES), cols_at, rows_at, trans_count, band, trans)
    got = exchange(send, "chip")
    mate = swap_cores(got)
    share, code = call(
        meet_kernel,
        [VMEM, VMEM, VMEM, VMEM, SMEM, VMEM, VMEM],
        [share_like, floats(2, chips, LANES)],
        [wide_scr, cols_scr, half_scr],
    )(own, part, got, mate, info, band, trans)
    shares = exchange(share, LOCAL)
    ext, first, send, part = call(
        second_kernel,
        [VMEM, VMEM, SMEM, VMEM, VMEM],
        [floats(16, width), own_like, floats(STEP * chips, LANES), floats(2 * blk_g, width)],
        [cols_scr, wide_scr, half_scr, half_scr],
    )(shares, code, info, band, trans)
    got = exchange(send.reshape(STEP * chips // 2, 2, LANES), "chip").reshape(send.shape)
    (share,) = call(
        third_kernel,
        [VMEM, VMEM, VMEM, VMEM, SMEM, VMEM, VMEM],
        [share_like],
        [wide_scr, cols_scr, half_scr],
    )(code, got, ext, part, info, band, trans)
    shares = exchange(share, LOCAL)
    second, stats = call(
        stats_kernel, [VMEM] * 4, [own_like, floats(2 * chips, LANES)]
    )(shares, own, ext, first)
    stats = exchange(stats, GENOME)
    weights, coverage = call(
        final_kernel, [VMEM] * 4, [floats(2 * blk_g, LANES)] * 2
    )(stats, own, ext, second)
    return (weights.reshape(-1), coverage.reshape(-1))


GENOME = ("chip", "core")
LOCAL = ("core", "rep")
STEP = 10


def solution(mesh):
    names = mesh.axis_names
    groups, replicas = (mesh.shape[name] for name in ("genome", "rep"))
    assert names == ("genome", "rep")
    devices = mesh.devices.reshape(groups // 2, 2, replicas)
    split = Mesh(devices, GENOME + ("rep",))
    every = P(GENOME + ("rep",))
    out_specs = (P(GENOME), P(GENOME))
    return jax.shard_map(
        shards, mesh=split, in_specs=(every,) * 5 + (P(GENOME),), out_specs=out_specs, check_vma=False
    )
```

```python
import functools

import jax
import jax.numpy as jnp
from jax import lax
from jax.experimental import pallas as pl
from jax.experimental.pallas import tpu as pltpu
from jax.sharding import Mesh, PartitionSpec as P

F32 = jnp.float32
I32 = jnp.int32
LANES = 128
CHUNK = 32
VMEM = pl.BlockSpec(memory_space=pltpu.VMEM)
SMEM = pl.BlockSpec(memory_space=pltpu.SMEM)
HBM = pl.BlockSpec(memory_space=pltpu.HBM)
ANY = pl.BlockSpec(memory_space=pl.ANY)


def rows_iota(shape):
    return lax.broadcasted_iota(I32, shape, 0)


def lanes_iota(shape):
    return lax.broadcasted_iota(I32, shape, 1)


def columns_of(block_rows):
    n, width = block_rows.shape
    padded = jnp.concatenate([block_rows, jnp.zeros((LANES - n, width), F32)], axis=0)
    return jnp.transpose(padded)


def pick_lane(ref, start, lane):
    chunk = ref[start : start + CHUNK, :]
    return jnp.sum(jnp.where(lanes_iota(chunk.shape) == lane, chunk, 0.0), axis=1, keepdims=True)


def fold(chunk):
    total = chunk[0:8]
    for at in range(8, chunk.shape[0], 8):
        total = total + chunk[at : at + 8]
    return total


def put_lane(ref, start, lane, column):
    hit = lanes_iota((CHUNK, LANES)) == lane
    ref[start : start + CHUNK, :] += jnp.where(hit, column, 0.0)


def band_columns(band_ref, cols_scr, sums_scr, anchor, ready):
    blk_dev, spans, width, _ = band_ref.shape
    sums_scr[...] = jnp.zeros(sums_scr.shape, F32)

    def one(q, carry):
        ready(q)
        sums = [jnp.zeros((8, width), F32) for _ in range(spans)]
        for start in range(0, width, CHUNK):
            here = pick_lane(cols_scr, start, anchor + q)
            for k in range(spans):
                chunk = band_ref[q, k, start : start + CHUNK, :]
                if k == 0:
                    above = rows_iota(chunk.shape) + start < lanes_iota(chunk.shape)
                    chunk = jnp.where(above, chunk, 0.0)
                sums[k] = sums[k] + fold(chunk * here)
        for k in range(spans):
            sums_scr[pl.ds(anchor + q + k, 1), :] += jnp.sum(sums[k], axis=0, keepdims=True)
        return carry

    lax.fori_loop(0, blk_dev, one, 0, unroll=True)


def band_rows(band_ref, ext_scr, racc_scr, anchor):
    blk_dev, spans, width, _ = band_ref.shape

    def one(q, carry):
        biases = [ext_scr[pl.ds(anchor + q + k, 1), :] for k in range(spans)]
        for start in range(0, width, CHUNK):
            total = jnp.zeros((CHUNK, width), F32)
            for k in range(spans):
                chunk = band_ref[q, k, start : start + CHUNK, :]
                if k == 0:
                    upper = rows_iota(chunk.shape) + start <= lanes_iota(chunk.shape)
                    chunk = jnp.where(upper, chunk, 0.0)
                total = total + chunk * biases[k]
            put_lane(racc_scr, start, anchor + q, jnp.sum(total, axis=1, keepdims=True))
        return carry

    lax.fori_loop(0, blk_dev, one, 0, unroll=True)


def trans_columns(trans_ref, info_ref, cols_scr, emit, ready):
    tiles, width, _ = trans_ref.shape

    def one(t, carry):
        ready(t)
        total = jnp.zeros((8, width), F32)
        for start in range(0, width, CHUNK):
            here = pick_lane(cols_scr, start, info_ref[8 + t])
            total = total + fold(trans_ref[t, start : start + CHUNK, :] * here)
        emit(t, jnp.sum(total, axis=0, keepdims=True))
        return carry

    lax.fori_loop(0, tiles, one, 0, unroll=True)


def trans_rows(trans_ref, info_ref, bias_of, racc_scr):
    tiles, width, _ = trans_ref.shape

    def one(t, carry):
        near, far = bias_of(t)
        for start in range(0, width, CHUNK):
            chunk = trans_ref[t, start : start + CHUNK, :]
            total = chunk[:, :LANES] * near + chunk[:, LANES:] * far
            put_lane(racc_scr, start, info_ref[8 + t], jnp.sum(total, axis=1, keepdims=True))
        return carry

    lax.fori_loop(0, tiles, one, 0, unroll=True)


def add_sums(code_of, half_of, steps, blk_g):
    out = [[jnp.zeros((8, LANES), F32) for _ in range(2)] for _ in range(blk_g)]
    for step in steps:
        code = code_of(step)
        for h in range(2):
            piece = half_of(step, h)
            for c in range(blk_g):
                out[c][h] = out[c][h] + jnp.where(code == c + 1.0, piece, 0.0)
    sums = [[jnp.sum(half, axis=0, keepdims=True) for half in pair] for pair in out]
    return jnp.concatenate([jnp.concatenate(pair, axis=1) for pair in sums], axis=0)


def nothing(_):
    pass


def quotient(value, size):
    if size & (size - 1):
        return lax.div(value, size)
    return lax.shift_right_logical(value, size.bit_length() - 1)


def fill_send(bias, info_ref, band_ref, trans_ref, send_ref, part_ref, scratch, band_ready,
              trans_ready):
    cols_scr, sums_scr, flat_scr, spill_scr = scratch
    blk_g = bias.shape[0]
    blk_dev, spans = band_ref.shape[:2]
    slot = 2 * blk_g
    half = slot // 2
    reach = spans - 1
    chip, core = lax.axis_index("chip"), lax.axis_index("core")
    here = 2 * chip + core
    for h in range(2):
        flat_scr[pl.ds(h, blk_g, stride=2), :] = bias[:, LANES * h : LANES * h + LANES]
    cols_scr[...] = columns_of(bias)
    flat = flat_scr[...]
    for at in range(send_ref.shape[0] // slot):
        send_ref[slot * at : slot * at + slot, :] = jnp.where(at < chip, flat, 0.0)

    def emit(t, sums):
        base = slot * quotient(info_ref[t], 2)
        odd = info_ref[t] & 1
        code = jnp.where(info_ref[t] == here, 0, info_ref[16 + t] + 1).astype(F32)
        for h in range(2):
            send_ref[pl.ds(base + 2 * odd + h, 1), :] = sums[:, LANES * h : LANES * h + LANES]
        send_ref[pl.ds(base + 4 + odd, 1), :] = jnp.full((1, LANES), code, F32)

    trans_columns(trans_ref, info_ref, cols_scr, emit, trans_ready)
    anchor = lax.axis_index("rep") * blk_dev
    band_columns(band_ref, cols_scr, sums_scr, anchor, band_ready)
    part_ref[...] = sums_scr[0:blk_g, :]
    for h in range(2):
        part = sums_scr[blk_g : blk_g + reach, LANES * h : LANES * h + LANES]
        spill_scr[pl.ds(h, reach, stride=2), :] = part
    spill = spill_scr[...]
    mine = pl.multiple_of(slot * chip, slot)
    send_ref[pl.ds(mine, half), :] = flat[0:half]
    send_ref[pl.ds(mine + half, half), :] = spill

    @pl.when((core == 1) & (chip < lax.axis_size("chip") - 1))
    def _():
        send_ref[pl.ds(mine + slot + half, half), :] = spill


def first_kernel(count_ref, masked_in, cols_in, rows_in, band_in, trans_in, own_ref, info_ref, send_ref,
                 part_ref, band_ref, trans_ref, masked_ref, cols_ref, rows_ref, sems, tile_sems,
                 flat_scr, *scratch):
    blk_g = own_ref.shape[0]
    blk_dev, tiles = band_ref.shape[0], trans_ref.shape[0]
    small = [
        pltpu.make_async_copy(src, dst, sems.at[i])
        for i, (src, dst) in enumerate(
            ((cols_in, cols_ref), (rows_in, rows_ref), (masked_in, masked_ref))
        )
    ]

    some = tiles // 2 if tiles % 2 == 0 else tiles

    def trans_copy(i):
        part = pl.ds(some * i, some)
        return pltpu.make_async_copy(trans_in.at[part], trans_ref.at[part], tile_sems.at[i])

    def band_copy(q):
        return pltpu.make_async_copy(band_in.at[q], band_ref.at[q], tile_sems.at[tiles + q])

    for copy in small:
        copy.start()
    for i in range(tiles // some):
        trans_copy(i).start(priority=i % 2)
    for q in range(blk_dev):
        band_copy(q).start(priority=q % 2)
    for copy in small:
        copy.wait()
    here = 2 * lax.axis_index("chip") + lax.axis_index("core")
    for t in range(tiles):
        used = t < count_ref[0]
        target = quotient(cols_ref[t], blk_g)
        info_ref[t] = jnp.where(used, target, here)
        info_ref[8 + t] = jnp.where(used, rows_ref[t] - here * blk_g, LANES - 1)
        info_ref[16 + t] = cols_ref[t] - target * blk_g
    flat_scr[...] = 1.0 - masked_ref[...].astype(F32)
    own = jnp.concatenate([flat_scr[pl.ds(h, blk_g, stride=2), :] for h in range(2)], axis=1)
    own_ref[...] = own

    def trans_ready(t):
        @pl.when(t % some == 0)
        def _():
            trans_copy(t // some).wait()

    fill_send(own, info_ref, band_ref, trans_ref, send_ref, part_ref, scratch,
              lambda q: band_copy(q).wait(), trans_ready)


def spread(value, scr):
    scr[...] = value
    n = value.shape[0] // 2
    return jnp.concatenate([scr[pl.ds(h, n, stride=2), :] for h in range(2)], axis=1)


def meet_kernel(own_ref, part_ref, got_ref, mate_ref, info_in, band_ref, trans_ref,
                share_ref, code_ref, info_ref, info_sem, ext_scr, racc_scr, near_scr):
    table = pltpu.make_async_copy(info_in, info_ref, info_sem)
    table.start()
    blk_g, width = own_ref.shape
    blk_dev, spans = band_ref.shape[:2]
    reach = spans - 1
    slot = 2 * blk_g
    half = slot // 2
    chips = got_ref.shape[0] // slot
    chip, core = lax.axis_index("chip"), lax.axis_index("core")
    anchor = lax.axis_index("rep") * blk_dev
    first = core == 0
    at = pl.multiple_of(slot * jnp.minimum(chip + core, chips - 1), slot)
    ahead = jnp.where(chip + core < chips, mate_ref[pl.ds(at, half), :], 0.0)
    at = pl.multiple_of(slot * jnp.maximum(chip + core - 1, 0), slot)
    back = jnp.where(chip + core > 0, mate_ref[pl.ds(at + half, half), :], 0.0)
    ext_scr[0:blk_g, :] = own_ref[...]
    ext_scr[blk_g : blk_g + reach, :] = spread(ahead, near_scr)
    racc_scr[...] = jnp.zeros(racc_scr.shape, F32)
    band_rows(band_ref, ext_scr, racc_scr, anchor)
    table.wait()

    def bias_of(t):
        source = info_ref[t]
        row = slot * quotient(source, 2) + 2 * info_ref[16 + t]
        same = (source & 1) == core
        return [
            jnp.where(same, got_ref[pl.ds(row + h, 1), :], mate_ref[pl.ds(row + h, 1), :])
            for h in range(2)
        ]

    trans_rows(trans_ref, info_ref, bias_of, racc_scr)

    def pick(ref, step, row):
        even, odd = row
        base = step * 8 * slot
        return jnp.where(
            first,
            ref[pl.ds(base + even, 8, stride=slot), :],
            ref[pl.ds(base + odd, 8, stride=slot), :],
        )

    steps = [(i, step) for i in range(2) for step in range(chips // 8)]
    refs = (got_ref, mate_ref)

    def code_of(which):
        i, step = which
        code = pick(refs[i], step, (4, 5))
        return jnp.where(rows_iota(code.shape) + 8 * step < chip, code, 0.0)

    sums = add_sums(code_of, lambda w, h: pick(refs[w[0]], w[1], (h, 2 + h)), steps, blk_g)
    for i in range(2):
        code = got_ref[pl.ds(4 + i, chips, stride=slot), :]
        code_ref[i] = jnp.where(rows_iota(code.shape) < chip, code, 0.0)
    total = part_ref[...] + jnp.transpose(racc_scr[...])[0:blk_g, :] + sums
    total = total + jnp.concatenate(
        [spread(back, near_scr), jnp.zeros((blk_g - reach, width), F32)], axis=0
    )
    total = jnp.where(own_ref[...] > 0.0, total, jnp.inf)
    for s in range(share_ref.shape[0]):
        share_ref[s] = total


def halves(block):
    return [block[:, LANES * h : LANES * h + LANES] for h in range(2)]


def second_kernel(shares_ref, code_ref, info_in, band_ref, trans_ref, ext_ref, first_ref, send_ref,
                  part_ref, info_ref, info_sem, cols_scr, sums_scr, spill_scr, ahead_scr):
    table = pltpu.make_async_copy(info_in, info_ref, info_sem)
    table.start()
    blk_g = first_ref.shape[0]
    blk_dev, spans = band_ref.shape[:2]
    reach = spans - 1
    replicas = shares_ref.shape[0] // 2
    chips = send_ref.shape[0] // STEP
    chip, core = lax.axis_index("chip"), lax.axis_index("core")
    first = core == 0
    totals, biases = [], []
    for c in range(2):
        total = shares_ref[c * replicas]
        for s in range(1, replicas):
            total = total + shares_ref[c * replicas + s]
        kept = total != jnp.inf
        totals.append(jnp.where(kept, total, 0.0))
        biases.append(jnp.where(kept, 1.0 / jnp.where(kept, total, 1.0), 0.0))
    first_ref[...] = jnp.where(first, totals[0], totals[1])
    own = jnp.where(first, biases[0], biases[1])
    ext_ref[0:blk_g, :] = own
    ext_ref[blk_g : blk_g + reach, :] = biases[1][0:reach]
    ext_ref[blk_g + reach :, :] = jnp.zeros((ext_ref.shape[0] - blk_g - reach, own.shape[1]), F32)
    cols_scr[...] = columns_of(own)
    for i in range(2):
        pieces = halves(biases[i])
        for at in range(0, chips, 8):
            code = code_ref[i, at : at + 8, :]
            for h in range(2):
                piece = jnp.zeros((8, LANES), F32)
                for c in range(blk_g):
                    piece = jnp.where(code == c + 1.0, pieces[h][c : c + 1], piece)
                send_ref[pl.ds(STEP * at + 2 - 2 * i + h, 8, stride=STEP), :] = piece

    def emit(t, sums):
        base = STEP * quotient(info_ref[t], 2) + 2 - 2 * (info_ref[t] & 1)
        for h in range(2):
            send_ref[pl.ds(base + h, 1), :] = halves(sums)[h]

    band_columns(band_ref, cols_scr, sums_scr, lax.axis_index("rep") * blk_dev, nothing)
    table.wait()
    trans_columns(trans_ref, info_ref, cols_scr, emit, nothing)
    spill = sums_scr[blk_g : blk_g + reach, :]
    part_ref[0:blk_g, :] = sums_scr[0:blk_g, :]
    mate = jnp.concatenate([spill, jnp.zeros((blk_g - reach, own.shape[1]), F32)], axis=0)
    part_ref[blk_g : 2 * blk_g, :] = jnp.where(first, mate, 0.0)
    for h in range(2):
        spill_scr[pl.ds(h, reach, stride=2), :] = halves(spill)[h]
        ahead_scr[pl.ds(h, reach, stride=2), :] = halves(biases[0])[h][0:reach]

    @pl.when((core == 1) & (chip > 0))
    def _():
        for i in range(2 * reach):
            send_ref[pl.ds(STEP * (chip - 1) + 2 + i, 1), :] = ahead_scr[i : i + 1, :]

    @pl.when((core == 1) & (chip < chips - 1))
    def _():
        for i in range(2 * reach):
            send_ref[pl.ds(STEP * (chip + 1) + 2 + i, 1), :] = spill_scr[i : i + 1, :]


def third_kernel(code_ref, got_ref, ext_ref, part_ref, info_in, band_ref, trans_ref, share_ref,
                 info_ref, info_sem, ext_scr, racc_scr, near_scr):
    table = pltpu.make_async_copy(info_in, info_ref, info_sem)
    table.start()
    blk_g = part_ref.shape[0] // 2
    blk_dev, spans = band_ref.shape[:2]
    reach = spans - 1
    replicas = share_ref.shape[0] // 2
    chips = got_ref.shape[0] // STEP
    chip, core = lax.axis_index("chip"), lax.axis_index("core")
    first = core == 0
    ext_scr[...] = ext_ref[...]
    racc_scr[...] = jnp.zeros(racc_scr.shape, F32)

    def edge(at, valid):
        at = jnp.clip(at, 0, chips - 1)
        for i in range(2 * reach):
            near_scr[i : i + 1, :] = got_ref[pl.ds(STEP * at + 2 + i, 1), :]
        block = jnp.concatenate([near_scr[pl.ds(h, reach, stride=2), :] for h in range(2)], axis=1)
        return jnp.where(valid, block, 0.0)

    ahead = edge(chip + 1, chip + 1 < chips)
    ext_scr[blk_g : blk_g + reach, :] = jnp.where(first, ext_ref[blk_g : blk_g + reach, :], ahead)
    back = edge(chip - 1, (core == 1) & (chip > 0))
    band_rows(band_ref, ext_scr, racc_scr, lax.axis_index("rep") * blk_dev)
    table.wait()

    def bias_of(t):
        base = STEP * quotient(info_ref[t], 2) + 2 - 2 * (info_ref[t] & 1)
        return [got_ref[pl.ds(base + h, 1), :] for h in range(2)]

    trans_rows(trans_ref, info_ref, bias_of, racc_scr)
    sums = [
        add_sums(
            lambda at: code_ref[i, at : at + 8, :],
            lambda at, h: got_ref[pl.ds(STEP * at + 2 - 2 * i + h, 8, stride=STEP), :],
            range(0, chips, 8),
            blk_g,
        )
        for i in range(2)
    ]
    own = part_ref[0:blk_g, :] + jnp.transpose(racc_scr[...])[0:blk_g, :]
    own = own + jnp.where(first, sums[0], sums[1])
    mate = part_ref[blk_g : 2 * blk_g, :] + jnp.where(first, sums[1], sums[0])
    mate = mate + jnp.concatenate([back, jnp.zeros((blk_g - reach, own.shape[1]), F32)], axis=0)
    for c in range(2):
        block = jnp.where(core == c, own, mate)
        for s in range(replicas):
            share_ref[c * replicas + s] = block


def whole_sum(block):
    return jnp.sum(jnp.sum(block, axis=0, keepdims=True), axis=1, keepdims=True)


def stats_kernel(shares_ref, own_ref, ext_ref, first_ref, second_ref, stats_ref):
    bias = ext_ref[0 : own_ref.shape[0], :]
    total = shares_ref[0]
    for s in range(1, shares_ref.shape[0]):
        total = total + shares_ref[s]
    second_ref[...] = total
    count = whole_sum(own_ref[...])
    sum_one = whole_sum(first_ref[...])
    scale = sum_one / jnp.maximum(count, 1.0)
    scale = jnp.where(scale == 0.0, 1.0, scale)
    sum_two = whole_sum((bias * scale) * (total * scale))
    lane = lanes_iota(stats_ref.shape)
    stats = jnp.where(lane == 0, sum_one, 0.0)
    stats = jnp.where(lane == 1, sum_two, stats)
    stats = jnp.where(lane == 2, scale, stats)
    stats_ref[...] = jnp.where(lane == 3, count, stats)


def final_kernel(stats_ref, own_ref, ext_ref, second_ref, weights_ref, coverage_ref):
    stats = stats_ref[...]
    lane = lanes_iota(stats.shape)

    def lane_of(at):
        return jnp.sum(jnp.where(lane == at, stats, 0.0), axis=1, keepdims=True)

    count = jnp.sum(lane_of(3), axis=0, keepdims=True)
    average_one = jnp.sum(lane_of(0), axis=0, keepdims=True) / count
    ratio = average_one / lane_of(2)
    average_two = jnp.sum(lane_of(1) * ratio * ratio, axis=0, keepdims=True) / count
    own = own_ref[...]
    blk_g = own.shape[0]
    kept = own > 0.0
    total = second_ref[...] * average_one
    coverage = (ext_ref[0:blk_g, :] * average_one) * total
    weights = jnp.where(kept, average_two / jnp.where(kept, total, 1.0), 0.0)
    for h in range(2):
        part = slice(LANES * h, LANES * h + LANES)
        weights_ref[pl.ds(h, blk_g, stride=2), :] = weights[:, part]
        coverage_ref[pl.ds(h, blk_g, stride=2), :] = coverage[:, part]


def call(kernel, ins, outs, scratch=(), cost=None, limit=16):
    return pl.pallas_call(
        kernel,
        in_specs=list(ins),
        out_shape=[jax.ShapeDtypeStruct(s, d) for s, d, _ in outs],
        out_specs=[spec for _, _, spec in outs],
        scratch_shapes=list(scratch),
        compiler_params=pltpu.CompilerParams(vmem_limit_bytes=limit * 1024 * 1024),
        cost_estimate=cost and pl.CostEstimate(flops=cost, bytes_accessed=cost, transcendentals=0),
    )


def floats(*shape):
    return (shape, F32, VMEM)


def exchange(block, axis):
    return lax.all_to_all(block, axis, 0, 0, tiled=True)


def swap_cores(block):
    return lax.ppermute(block, "core", [(0, 1), (1, 0)])


def shards(band, trans, rows_at, cols_at, trans_count, masked):
    blk_dev, spans, width, _ = band.shape
    tiles = trans.shape[0]
    replicas = lax.axis_size("rep")
    chips = lax.axis_size("chip")
    blk_g = blk_dev * replicas
    own_like = floats(blk_g, width)
    send_like = floats(chips * 2 * blk_g, LANES)
    share_like = floats(2 * replicas, blk_g, width)
    cols_scr = pltpu.VMEM((width, LANES), F32)
    wide_scr = pltpu.VMEM((16, width), F32)
    flat_scr = pltpu.VMEM((2 * blk_g, LANES), F32)
    half_scr = pltpu.VMEM((2 * spans - 2, LANES), F32)
    info_scr = [pltpu.SMEM((24,), I32), pltpu.SemaphoreType.DMA(())]
    fill_scr = [cols_scr, wide_scr, flat_scr, half_scr]
    masked, cols_at, rows_at, band, trans = (
        pltpu.with_memory_space_constraint(x, pltpu.HBM)
        for x in (masked.reshape(2 * blk_g, LANES), cols_at, rows_at, band, trans)
    )
    own, info, send, part, band, trans = pl.pallas_call(
        first_kernel,
        in_specs=[SMEM] + [HBM] * 5,
        out_shape=[
            jax.ShapeDtypeStruct((blk_g, width), F32),
            jax.ShapeDtypeStruct((24,), I32),
            jax.ShapeDtypeStruct((chips * 2 * blk_g, LANES), F32),
            jax.ShapeDtypeStruct((blk_g, width), F32),
            pltpu.VMEM(band.shape, F32),
            pltpu.VMEM(trans.shape, F32),
        ],
        out_specs=[VMEM, SMEM, VMEM, VMEM, VMEM, VMEM],
        scratch_shapes=[
            pltpu.VMEM((2 * blk_g, LANES), I32),
            pltpu.SMEM((tiles,), I32),
            pltpu.SMEM((tiles,), I32),
            pltpu.SemaphoreType.DMA((3,)),
            pltpu.SemaphoreType.DMA((tiles + blk_dev,)),
            flat_scr,
        ] + fill_scr,
        compiler_params=pltpu.CompilerParams(vmem_limit_bytes=16 * 1024 * 1024),
    )(trans_count, masked, cols_at, rows_at, band, trans)
    got = exchange(send, "chip")
    mate = swap_cores(got)
    share, code = call(
        meet_kernel,
        [VMEM, VMEM, VMEM, VMEM, ANY, VMEM, VMEM],
        [share_like, floats(2, chips, LANES)],
        info_scr + [wide_scr, cols_scr, half_scr],
    )(own, part, got, mate, info, band, trans)
    shares = exchange(share, LOCAL)
    ext, first, send, part = call(
        second_kernel,
        [VMEM, VMEM, ANY, VMEM, VMEM],
        [floats(16, width), own_like, floats(STEP * chips, LANES), floats(2 * blk_g, width)],
        info_scr + [cols_scr, wide_scr, half_scr, half_scr],
    )(shares, code, info, band, trans)
    got = exchange(send.reshape(STEP * chips // 2, 2, LANES), "chip").reshape(send.shape)
    (share,) = call(
        third_kernel,
        [VMEM, VMEM, VMEM, VMEM, ANY, VMEM, VMEM],
        [share_like],
        info_scr + [wide_scr, cols_scr, half_scr],
    )(code, got, ext, part, info, band, trans)
    shares = exchange(share, LOCAL)
    second, stats = call(
        stats_kernel, [VMEM] * 4, [own_like, floats(2 * chips, LANES)]
    )(shares, own, ext, first)
    stats = exchange(stats, GENOME)
    weights, coverage = call(
        final_kernel, [VMEM] * 4, [floats(2 * blk_g, LANES)] * 2
    )(stats, own, ext, second)
    return (weights.reshape(-1), coverage.reshape(-1))


GENOME = ("chip", "core")
LOCAL = ("core", "rep")
STEP = 10


def solution(mesh):
    names = mesh.axis_names
    groups, replicas = (mesh.shape[name] for name in ("genome", "rep"))
    assert names == ("genome", "rep")
    devices = mesh.devices.reshape(groups // 2, 2, replicas)
    split = Mesh(devices, GENOME + ("rep",))
    every = P(GENOME + ("rep",))
    out_specs = (P(GENOME), P(GENOME))
    return jax.shard_map(
        shards, mesh=split, in_specs=(every,) * 5 + (P(GENOME),), out_specs=out_specs, check_vma=False
    )
```

```python
import functools

import jax
import jax.numpy as jnp
from jax import lax
from jax.experimental import pallas as pl
from jax.experimental.pallas import tpu as pltpu
from jax.sharding import Mesh, PartitionSpec as P

F32 = jnp.float32
I32 = jnp.int32
LANES = 128
CHUNK = 32
VMEM = pl.BlockSpec(memory_space=pltpu.VMEM)
SMEM = pl.BlockSpec(memory_space=pltpu.SMEM)
HBM = pl.BlockSpec(memory_space=pltpu.HBM)
ANY = pl.BlockSpec(memory_space=pl.ANY)


def rows_iota(shape):
    return lax.broadcasted_iota(I32, shape, 0)


def lanes_iota(shape):
    return lax.broadcasted_iota(I32, shape, 1)


def columns_of(block_rows):
    n, width = block_rows.shape
    padded = jnp.concatenate([block_rows, jnp.zeros((LANES - n, width), F32)], axis=0)
    return jnp.transpose(padded)


def pick_lane(ref, start, lane):
    chunk = ref[start : start + CHUNK, :]
    return jnp.sum(jnp.where(lanes_iota(chunk.shape) == lane, chunk, 0.0), axis=1, keepdims=True)


def fold(chunk):
    total = chunk[0:8]
    for at in range(8, chunk.shape[0], 8):
        total = total + chunk[at : at + 8]
    return total


def put_lane(ref, start, lane, column):
    hit = lanes_iota((CHUNK, LANES)) == lane
    ref[start : start + CHUNK, :] += jnp.where(hit, column, 0.0)


def band_columns(band_ref, cols_scr, sums_scr, anchor, ready):
    blk_dev, spans, width, _ = band_ref.shape
    sums_scr[...] = jnp.zeros(sums_scr.shape, F32)

    def one(q, carry):
        ready(q)
        sums = [jnp.zeros((8, width), F32) for _ in range(spans)]
        for start in range(0, width, CHUNK):
            here = pick_lane(cols_scr, start, anchor + q)
            for k in range(spans):
                chunk = band_ref[q, k, start : start + CHUNK, :]
                if k == 0:
                    above = rows_iota(chunk.shape) + start < lanes_iota(chunk.shape)
                    chunk = jnp.where(above, chunk, 0.0)
                sums[k] = sums[k] + fold(chunk * here)
        for k in range(spans):
            sums_scr[pl.ds(anchor + q + k, 1), :] += jnp.sum(sums[k], axis=0, keepdims=True)
        return carry

    lax.fori_loop(0, blk_dev, one, 0, unroll=True)


def band_rows(band_ref, ext_scr, racc_scr, anchor):
    blk_dev, spans, width, _ = band_ref.shape

    def one(q, carry):
        biases = [ext_scr[pl.ds(anchor + q + k, 1), :] for k in range(spans)]
        for start in range(0, width, CHUNK):
            total = jnp.zeros((CHUNK, width), F32)
            for k in range(spans):
                chunk = band_ref[q, k, start : start + CHUNK, :]
                if k == 0:
                    upper = rows_iota(chunk.shape) + start <= lanes_iota(chunk.shape)
                    chunk = jnp.where(upper, chunk, 0.0)
                total = total + chunk * biases[k]
            put_lane(racc_scr, start, anchor + q, jnp.sum(total, axis=1, keepdims=True))
        return carry

    lax.fori_loop(0, blk_dev, one, 0, unroll=True)


def trans_columns(trans_ref, info_ref, cols_scr, emit, ready):
    tiles, width, _ = trans_ref.shape

    def one(t, carry):
        ready(t)
        total = jnp.zeros((8, width), F32)
        for start in range(0, width, CHUNK):
            here = pick_lane(cols_scr, start, info_ref[8 + t])
            total = total + fold(trans_ref[t, start : start + CHUNK, :] * here)
        emit(t, jnp.sum(total, axis=0, keepdims=True))
        return carry

    lax.fori_loop(0, tiles, one, 0, unroll=True)


def trans_rows(trans_ref, info_ref, bias_of, racc_scr):
    tiles, width, _ = trans_ref.shape

    def one(t, carry):
        near, far = bias_of(t)
        for start in range(0, width, CHUNK):
            chunk = trans_ref[t, start : start + CHUNK, :]
            total = chunk[:, :LANES] * near + chunk[:, LANES:] * far
            put_lane(racc_scr, start, info_ref[8 + t], jnp.sum(total, axis=1, keepdims=True))
        return carry

    lax.fori_loop(0, tiles, one, 0, unroll=True)


def add_sums(code_of, half_of, steps, blk_g):
    out = [[jnp.zeros((8, LANES), F32) for _ in range(2)] for _ in range(blk_g)]
    for step in steps:
        code = code_of(step)
        for h in range(2):
            piece = half_of(step, h)
            for c in range(blk_g):
                out[c][h] = out[c][h] + jnp.where(code == c + 1.0, piece, 0.0)
    sums = [[jnp.sum(half, axis=0, keepdims=True) for half in pair] for pair in out]
    return jnp.concatenate([jnp.concatenate(pair, axis=1) for pair in sums], axis=0)


def nothing(_):
    pass


def quotient(value, size):
    if size & (size - 1):
        return lax.div(value, size)
    return lax.shift_right_logical(value, size.bit_length() - 1)


def fill_send(bias, info_ref, band_ref, trans_ref, send_ref, part_ref, scratch, band_ready,
              trans_ready):
    cols_scr, sums_scr, flat_scr, spill_scr = scratch
    blk_g = bias.shape[0]
    blk_dev, spans = band_ref.shape[:2]
    slot = 2 * blk_g
    half = slot // 2
    reach = spans - 1
    chip, core = lax.axis_index("chip"), lax.axis_index("core")
    here = 2 * chip + core
    for h in range(2):
        flat_scr[pl.ds(h, blk_g, stride=2), :] = bias[:, LANES * h : LANES * h + LANES]
    cols_scr[...] = columns_of(bias)
    flat = flat_scr[...]
    for at in range(send_ref.shape[0] // slot):
        send_ref[slot * at : slot * at + slot, :] = jnp.where(at < chip, flat, 0.0)

    def emit(t, sums):
        base = slot * quotient(info_ref[t], 2)
        odd = info_ref[t] & 1
        code = jnp.where(info_ref[t] == here, 0, info_ref[16 + t] + 1).astype(F32)
        for h in range(2):
            send_ref[pl.ds(base + 2 * odd + h, 1), :] = sums[:, LANES * h : LANES * h + LANES]
        send_ref[pl.ds(base + 4 + odd, 1), :] = jnp.full((1, LANES), code, F32)

    trans_columns(trans_ref, info_ref, cols_scr, emit, trans_ready)
    anchor = lax.axis_index("rep") * blk_dev
    band_columns(band_ref, cols_scr, sums_scr, anchor, band_ready)
    part_ref[...] = sums_scr[0:blk_g, :]
    for h in range(2):
        part = sums_scr[blk_g : blk_g + reach, LANES * h : LANES * h + LANES]
        spill_scr[pl.ds(h, reach, stride=2), :] = part
    spill = spill_scr[...]
    mine = pl.multiple_of(slot * chip, slot)
    send_ref[pl.ds(mine, half), :] = flat[0:half]
    send_ref[pl.ds(mine + half, half), :] = spill

    @pl.when((core == 1) & (chip < lax.axis_size("chip") - 1))
    def _():
        send_ref[pl.ds(mine + slot + half, half), :] = spill


def first_kernel(count_ref, masked_in, cols_in, rows_in, band_in, trans_in, own_ref, info_ref, send_ref,
                 part_ref, band_ref, trans_ref, masked_ref, cols_ref, rows_ref, sems, tile_sems,
                 flat_scr, *scratch):
    blk_g = own_ref.shape[0]
    blk_dev, tiles = band_ref.shape[0], trans_ref.shape[0]
    small = [
        pltpu.make_async_copy(src, dst, sems.at[i])
        for i, (src, dst) in enumerate(
            ((cols_in, cols_ref), (rows_in, rows_ref), (masked_in, masked_ref))
        )
    ]

    some = tiles // 2 if tiles % 2 == 0 else tiles

    def trans_copy(i):
        part = pl.ds(some * i, some)
        return pltpu.make_async_copy(trans_in.at[part], trans_ref.at[part], tile_sems.at[i])

    def band_copy(q):
        return pltpu.make_async_copy(band_in.at[q], band_ref.at[q], tile_sems.at[tiles + q])

    for copy in small:
        copy.start()
    for i in range(tiles // some):
        trans_copy(i).start(priority=i % 2)
    for q in range(blk_dev):
        band_copy(q).start(priority=q % 2)
    for copy in small:
        copy.wait()
    here = 2 * lax.axis_index("chip") + lax.axis_index("core")
    for t in range(tiles):
        used = t < count_ref[0]
        target = quotient(cols_ref[t], blk_g)
        info_ref[t] = jnp.where(used, target, here)
        info_ref[8 + t] = jnp.where(used, rows_ref[t] - here * blk_g, LANES - 1)
        info_ref[16 + t] = cols_ref[t] - target * blk_g
    flat_scr[...] = 1.0 - masked_ref[...].astype(F32)
    own = jnp.concatenate([flat_scr[pl.ds(h, blk_g, stride=2), :] for h in range(2)], axis=1)
    own_ref[...] = own

    def trans_ready(t):
        @pl.when(t % some == 0)
        def _():
            trans_copy(t // some).wait()

    fill_send(own, info_ref, band_ref, trans_ref, send_ref, part_ref, scratch,
              lambda q: band_copy(q).wait(), trans_ready)


def spread(value, scr):
    scr[...] = value
    n = value.shape[0] // 2
    return jnp.concatenate([scr[pl.ds(h, n, stride=2), :] for h in range(2)], axis=1)


def meet_kernel(own_ref, part_ref, got_ref, mate_ref, info_in, band_ref, trans_ref,
                share_ref, code_ref, info_ref, info_sem, ext_scr, racc_scr, near_scr):
    table = pltpu.make_async_copy(info_in, info_ref, info_sem)
    table.start()
    blk_g, width = own_ref.shape
    blk_dev, spans = band_ref.shape[:2]
    reach = spans - 1
    slot = 2 * blk_g
    half = slot // 2
    chips = got_ref.shape[0] // slot
    chip, core = lax.axis_index("chip"), lax.axis_index("core")
    anchor = lax.axis_index("rep") * blk_dev
    first = core == 0
    at = pl.multiple_of(slot * jnp.minimum(chip + core, chips - 1), slot)
    ahead = jnp.where(chip + core < chips, mate_ref[pl.ds(at, half), :], 0.0)
    at = pl.multiple_of(slot * jnp.maximum(chip + core - 1, 0), slot)
    back = jnp.where(chip + core > 0, mate_ref[pl.ds(at + half, half), :], 0.0)
    ext_scr[0:blk_g, :] = own_ref[...]
    ext_scr[blk_g : blk_g + reach, :] = spread(ahead, near_scr)
    racc_scr[...] = jnp.zeros(racc_scr.shape, F32)
    band_rows(band_ref, ext_scr, racc_scr, anchor)
    table.wait()

    def bias_of(t):
        source = info_ref[t]
        row = slot * quotient(source, 2) + 2 * info_ref[16 + t]
        same = (source & 1) == core
        return [
            jnp.where(same, got_ref[pl.ds(row + h, 1), :], mate_ref[pl.ds(row + h, 1), :])
            for h in range(2)
        ]

    trans_rows(trans_ref, info_ref, bias_of, racc_scr)

    def pick(ref, step, row):
        even, odd = row
        base = step * 8 * slot
        return jnp.where(
            first,
            ref[pl.ds(base + even, 8, stride=slot), :],
            ref[pl.ds(base + odd, 8, stride=slot), :],
        )

    steps = [(i, step) for i in range(2) for step in range(chips // 8)]
    refs = (got_ref, mate_ref)

    def code_of(which):
        i, step = which
        code = pick(refs[i], step, (4, 5))
        return jnp.where(rows_iota(code.shape) + 8 * step < chip, code, 0.0)

    sums = add_sums(code_of, lambda w, h: pick(refs[w[0]], w[1], (h, 2 + h)), steps, blk_g)
    for i in range(2):
        code = got_ref[pl.ds(4 + i, chips, stride=slot), :]
        code_ref[i] = jnp.where(rows_iota(code.shape) < chip, code, 0.0)
    total = part_ref[...] + jnp.transpose(racc_scr[...])[0:blk_g, :] + sums
    total = total + jnp.concatenate(
        [spread(back, near_scr), jnp.zeros((blk_g - reach, width), F32)], axis=0
    )
    total = jnp.where(own_ref[...] > 0.0, total, jnp.inf)
    for s in range(share_ref.shape[0]):
        share_ref[s] = total


def halves(block):
    return [block[:, LANES * h : LANES * h + LANES] for h in range(2)]


def whole_sum(block):
    return jnp.sum(jnp.sum(block, axis=0, keepdims=True), axis=1, keepdims=True)


def in_lanes(shape, *values):
    lane = lanes_iota(shape)
    out = jnp.zeros(shape, F32)
    for i, value in enumerate(values):
        out = jnp.where(lane == i, value, out)
    return out


def lane_of(block, at):
    return jnp.sum(jnp.where(lanes_iota(block.shape) == at, block, 0.0), axis=1, keepdims=True)


def second_kernel(shares_ref, code_ref, info_in, band_ref, trans_ref, ext_ref, first_ref, send_ref,
                  part_ref, info_ref, info_sem, cols_scr, sums_scr, spill_scr, ahead_scr):
    table = pltpu.make_async_copy(info_in, info_ref, info_sem)
    table.start()
    blk_g = shares_ref.shape[1]
    blk_dev, spans = band_ref.shape[:2]
    reach = spans - 1
    replicas = shares_ref.shape[0] // 2
    chips = send_ref.shape[0] // STEP
    chip, core = lax.axis_index("chip"), lax.axis_index("core")
    first = core == 0
    biases, sums, counts = [], [], []
    for c in range(2):
        total = shares_ref[c * replicas]
        for s in range(1, replicas):
            total = total + shares_ref[c * replicas + s]
        kept = total != jnp.inf
        sums.append(jnp.where(kept, total, 0.0))
        counts.append(jnp.where(kept, 1.0, 0.0))
        biases.append(jnp.where(kept, 1.0 / jnp.where(kept, total, 1.0), 0.0))
    sum_one, count = whole_sum(sums[0] + sums[1]), whole_sum(counts[0] + counts[1])
    scale = sum_one / jnp.maximum(count, 1.0)
    scale = jnp.where(scale == 0.0, 1.0, scale)
    first_ref[...] = in_lanes(first_ref.shape, sum_one, 0.0, scale, count)
    own = jnp.where(first, biases[0], biases[1])
    ext_ref[0:blk_g, :] = own
    ext_ref[blk_g:, :] = jnp.where(first, biases[1], biases[0])
    cols_scr[...] = columns_of(own)
    for i in range(2):
        pieces = halves(biases[i])
        for at in range(0, chips, 8):
            code = code_ref[i, at : at + 8, :]
            for h in range(2):
                piece = jnp.zeros((8, LANES), F32)
                for c in range(blk_g):
                    piece = jnp.where(code == c + 1.0, pieces[h][c : c + 1], piece)
                send_ref[pl.ds(STEP * at + 2 - 2 * i + h, 8, stride=STEP), :] = piece

    def emit(t, sums):
        base = STEP * quotient(info_ref[t], 2) + 2 - 2 * (info_ref[t] & 1)
        for h in range(2):
            send_ref[pl.ds(base + h, 1), :] = halves(sums)[h]

    band_columns(band_ref, cols_scr, sums_scr, lax.axis_index("rep") * blk_dev, nothing)
    table.wait()
    trans_columns(trans_ref, info_ref, cols_scr, emit, nothing)
    spill = sums_scr[blk_g : blk_g + reach, :]
    part_ref[0:blk_g, :] = sums_scr[0:blk_g, :]
    mate = jnp.concatenate([spill, jnp.zeros((blk_g - reach, own.shape[1]), F32)], axis=0)
    part_ref[blk_g : 2 * blk_g, :] = jnp.where(first, mate, 0.0)
    for h in range(2):
        spill_scr[pl.ds(h, reach, stride=2), :] = halves(spill)[h]
        ahead_scr[pl.ds(h, reach, stride=2), :] = halves(biases[0])[h][0:reach]

    @pl.when((core == 1) & (chip > 0))
    def _():
        for i in range(2 * reach):
            send_ref[pl.ds(STEP * (chip - 1) + 2 + i, 1), :] = ahead_scr[i : i + 1, :]

    @pl.when((core == 1) & (chip < chips - 1))
    def _():
        for i in range(2 * reach):
            send_ref[pl.ds(STEP * (chip + 1) + 2 + i, 1), :] = spill_scr[i : i + 1, :]


def third_kernel(code_ref, got_ref, ext_ref, part_ref, first_ref, info_in, band_ref, trans_ref, share_ref,
                 info_ref, info_sem, ext_scr, racc_scr, near_scr):
    table = pltpu.make_async_copy(info_in, info_ref, info_sem)
    table.start()
    blk_g = part_ref.shape[0] // 2
    blk_dev, spans = band_ref.shape[:2]
    reach = spans - 1
    replicas = share_ref.shape[0] // (2 * SHARE)
    chips = got_ref.shape[0] // STEP
    chip, core = lax.axis_index("chip"), lax.axis_index("core")
    first = core == 0
    ext_scr[...] = ext_ref[...]
    racc_scr[...] = jnp.zeros(racc_scr.shape, F32)

    def edge(at, valid):
        at = jnp.clip(at, 0, chips - 1)
        for i in range(2 * reach):
            near_scr[i : i + 1, :] = got_ref[pl.ds(STEP * at + 2 + i, 1), :]
        block = jnp.concatenate([near_scr[pl.ds(h, reach, stride=2), :] for h in range(2)], axis=1)
        return jnp.where(valid, block, 0.0)

    ahead = edge(chip + 1, chip + 1 < chips)
    ext_scr[blk_g : blk_g + reach, :] = jnp.where(first, ext_ref[blk_g : blk_g + reach, :], ahead)
    back = edge(chip - 1, (core == 1) & (chip > 0))
    band_rows(band_ref, ext_scr, racc_scr, lax.axis_index("rep") * blk_dev)
    table.wait()

    def bias_of(t):
        base = STEP * quotient(info_ref[t], 2) + 2 - 2 * (info_ref[t] & 1)
        return [got_ref[pl.ds(base + h, 1), :] for h in range(2)]

    trans_rows(trans_ref, info_ref, bias_of, racc_scr)
    sums = [
        add_sums(
            lambda at: code_ref[i, at : at + 8, :],
            lambda at, h: got_ref[pl.ds(STEP * at + 2 - 2 * i + h, 8, stride=STEP), :],
            range(0, chips, 8),
            blk_g,
        )
        for i in range(2)
    ]
    own = part_ref[0:blk_g, :] + jnp.transpose(racc_scr[...])[0:blk_g, :]
    own = own + jnp.where(first, sums[0], sums[1])
    mate = part_ref[blk_g : 2 * blk_g, :] + jnp.where(first, sums[1], sums[0])
    mate = mate + jnp.concatenate([back, jnp.zeros((blk_g - reach, own.shape[1]), F32)], axis=0)
    scale = lane_of(first_ref[0:1, :], 2)
    weighed = (ext_ref[0:blk_g, :] * scale) * (own * scale)
    sum_two = whole_sum(weighed + (ext_ref[blk_g:, :] * scale) * (mate * scale))
    for c in range(2):
        pieces = halves(jnp.where(core == c, own, mate))
        for s in range(replicas):
            at = SHARE * (c * replicas + s)
            for h in range(2):
                share_ref[pl.ds(at + h, blk_g, stride=2), :] = pieces[h]
            share_ref[at + 2 * blk_g : at + SHARE, :] = jnp.broadcast_to(sum_two, (2, LANES))


def stats_kernel(shares_ref, first_ref, second_ref, stats_ref):
    size = SHARE - 2
    shares = [shares_ref[at : at + SHARE, :] for at in range(0, shares_ref.shape[0], SHARE)]
    total = shares[0]
    for share in shares[1:]:
        total = total + share
    second_ref[...] = total[0:size]
    stats = jnp.where(lanes_iota((1, LANES)) == 1, total[size : size + 1], first_ref[0:1, :])
    stats_ref[...] = jnp.broadcast_to(stats, stats_ref.shape)


def final_kernel(stats_ref, own_ref, ext_ref, second_ref, weights_ref, coverage_ref):
    stats = stats_ref[...]
    count = jnp.sum(lane_of(stats, 3), axis=0, keepdims=True)
    average_one = jnp.sum(lane_of(stats, 0), axis=0, keepdims=True) / count
    ratio = average_one / lane_of(stats, 2)
    average_two = jnp.sum(lane_of(stats, 1) * ratio * ratio, axis=0, keepdims=True) / count
    blk_g = own_ref.shape[0]
    owns, biases = halves(own_ref[...]), halves(ext_ref[0:blk_g, :])
    for h in range(2):
        rows = pl.ds(h, blk_g, stride=2)
        kept = owns[h] > 0.0
        total = second_ref[rows, :] * average_one
        coverage_ref[rows, :] = (biases[h] * average_one) * total
        weights_ref[rows, :] = jnp.where(kept, average_two / jnp.where(kept, total, 1.0), 0.0)


def call(kernel, ins, outs, scratch=(), cost=None, limit=16):
    return pl.pallas_call(
        kernel,
        in_specs=list(ins),
        out_shape=[jax.ShapeDtypeStruct(s, d) for s, d, _ in outs],
        out_specs=[spec for _, _, spec in outs],
        scratch_shapes=list(scratch),
        compiler_params=pltpu.CompilerParams(vmem_limit_bytes=limit * 1024 * 1024),
        cost_estimate=cost and pl.CostEstimate(flops=cost, bytes_accessed=cost, transcendentals=0),
    )


def floats(*shape):
    return (shape, F32, VMEM)


def exchange(block, axis):
    return lax.all_to_all(block, axis, 0, 0, tiled=True)


def swap_cores(block):
    return lax.ppermute(block, "core", [(0, 1), (1, 0)])


def shards(band, trans, rows_at, cols_at, trans_count, masked):
    blk_dev, spans, width, _ = band.shape
    tiles = trans.shape[0]
    replicas = lax.axis_size("rep")
    chips = lax.axis_size("chip")
    blk_g = blk_dev * replicas
    own_like = floats(blk_g, width)
    send_like = floats(chips * 2 * blk_g, LANES)
    share_like = floats(2 * replicas, blk_g, width)
    cols_scr = pltpu.VMEM((width, LANES), F32)
    wide_scr = pltpu.VMEM((16, width), F32)
    flat_scr = pltpu.VMEM((2 * blk_g, LANES), F32)
    half_scr = pltpu.VMEM((2 * spans - 2, LANES), F32)
    info_scr = [pltpu.SMEM((24,), I32), pltpu.SemaphoreType.DMA(())]
    fill_scr = [cols_scr, wide_scr, flat_scr, half_scr]
    masked, cols_at, rows_at, band, trans = (
        pltpu.with_memory_space_constraint(x, pltpu.HBM)
        for x in (masked.reshape(2 * blk_g, LANES), cols_at, rows_at, band, trans)
    )
    own, info, send, part, band, trans = pl.pallas_call(
        first_kernel,
        in_specs=[SMEM] + [HBM] * 5,
        out_shape=[
            jax.ShapeDtypeStruct((blk_g, width), F32),
            jax.ShapeDtypeStruct((24,), I32),
            jax.ShapeDtypeStruct((chips * 2 * blk_g, LANES), F32),
            jax.ShapeDtypeStruct((blk_g, width), F32),
            pltpu.VMEM(band.shape, F32),
            pltpu.VMEM(trans.shape, F32),
        ],
        out_specs=[VMEM, SMEM, VMEM, VMEM, VMEM, VMEM],
        scratch_shapes=[
            pltpu.VMEM((2 * blk_g, LANES), I32),
            pltpu.SMEM((tiles,), I32),
            pltpu.SMEM((tiles,), I32),
            pltpu.SemaphoreType.DMA((3,)),
            pltpu.SemaphoreType.DMA((tiles + blk_dev,)),
            flat_scr,
        ] + fill_scr,
        compiler_params=pltpu.CompilerParams(vmem_limit_bytes=16 * 1024 * 1024),
    )(trans_count, masked, cols_at, rows_at, band, trans)
    got = exchange(send, "chip")
    mate = swap_cores(got)
    share, code = call(
        meet_kernel,
        [VMEM, VMEM, VMEM, VMEM, ANY, VMEM, VMEM],
        [share_like, floats(2, chips, LANES)],
        info_scr + [wide_scr, cols_scr, half_scr],
    )(own, part, got, mate, info, band, trans)
    shares = exchange(share, LOCAL)
    ext, first, send, part = call(
        second_kernel,
        [VMEM, VMEM, ANY, VMEM, VMEM],
        [floats(2 * blk_g, width), floats(8, LANES), floats(STEP * chips, LANES),
         floats(2 * blk_g, width)],
        info_scr + [cols_scr, wide_scr, half_scr, half_scr],
    )(shares, code, info, band, trans)
    got = exchange(send.reshape(STEP * chips // 2, 2, LANES), "chip").reshape(send.shape)
    (share,) = call(
        third_kernel,
        [VMEM, VMEM, VMEM, VMEM, VMEM, ANY, VMEM, VMEM],
        [floats(2 * replicas * SHARE, LANES)],
        info_scr + [wide_scr, cols_scr, half_scr],
    )(code, got, ext, part, first, info, band, trans)
    shares = exchange(share.reshape(replicas * SHARE, 2, LANES), LOCAL).reshape(share.shape)
    second, stats = call(
        stats_kernel, [VMEM, VMEM], [floats(2 * blk_g, LANES), floats(chips, LANES)]
    )(shares, first)
    stats = exchange(stats, "chip")
    weights, coverage = call(
        final_kernel, [VMEM] * 4, [floats(2 * blk_g, LANES)] * 2
    )(stats, own, ext, second)
    return (weights.reshape(-1), coverage.reshape(-1))


GENOME = ("chip", "core")
LOCAL = ("core", "rep")
STEP = 10
SHARE = 18


def solution(mesh):
    names = mesh.axis_names
    groups, replicas = (mesh.shape[name] for name in ("genome", "rep"))
    assert names == ("genome", "rep")
    devices = mesh.devices.reshape(groups // 2, 2, replicas)
    split = Mesh(devices, GENOME + ("rep",))
    every = P(GENOME + ("rep",))
    out_specs = (P(GENOME), P(GENOME))
    return jax.shard_map(
        shards, mesh=split, in_specs=(every,) * 5 + (P(GENOME),), out_specs=out_specs, check_vma=False
    )
```

```python
import functools

import jax
import jax.numpy as jnp
from jax import lax
from jax.experimental import pallas as pl
from jax.experimental.pallas import tpu as pltpu
from jax.sharding import Mesh, PartitionSpec as P

F32 = jnp.float32
I32 = jnp.int32
LANES = 128
CHUNK = 32
VMEM = pl.BlockSpec(memory_space=pltpu.VMEM)
SMEM = pl.BlockSpec(memory_space=pltpu.SMEM)
HBM = pl.BlockSpec(memory_space=pltpu.HBM)
ANY = pl.BlockSpec(memory_space=pl.ANY)


def rows_iota(shape):
    return lax.broadcasted_iota(I32, shape, 0)


def lanes_iota(shape):
    return lax.broadcasted_iota(I32, shape, 1)


def columns_of(block_rows):
    n, width = block_rows.shape
    padded = jnp.concatenate([block_rows, jnp.zeros((LANES - n, width), F32)], axis=0)
    return jnp.transpose(padded)


def pick_lane(ref, start, lane):
    chunk = ref[start : start + CHUNK, :]
    return jnp.sum(jnp.where(lanes_iota(chunk.shape) == lane, chunk, 0.0), axis=1, keepdims=True)


def fold(chunk):
    total = chunk[0:8]
    for at in range(8, chunk.shape[0], 8):
        total = total + chunk[at : at + 8]
    return total


def put_lane(ref, start, lane, column):
    hit = lanes_iota((CHUNK, LANES)) == lane
    ref[start : start + CHUNK, :] += jnp.where(hit, column, 0.0)


def band_columns(band_ref, cols_scr, sums_scr, anchor, ready):
    blk_dev, spans, width, _ = band_ref.shape
    sums_scr[...] = jnp.zeros(sums_scr.shape, F32)

    def one(q, carry):
        ready(q)
        sums = [jnp.zeros((8, width), F32) for _ in range(spans)]
        for start in range(0, width, CHUNK):
            here = pick_lane(cols_scr, start, anchor + q)
            for k in range(spans):
                chunk = band_ref[q, k, start : start + CHUNK, :]
                if k == 0:
                    above = rows_iota(chunk.shape) + start < lanes_iota(chunk.shape)
                    chunk = jnp.where(above, chunk, 0.0)
                sums[k] = sums[k] + fold(chunk * here)
        for k in range(spans):
            sums_scr[pl.ds(anchor + q + k, 1), :] += jnp.sum(sums[k], axis=0, keepdims=True)
        return carry

    lax.fori_loop(0, blk_dev, one, 0, unroll=True)


def band_rows(band_ref, ext_scr, racc_scr, anchor):
    blk_dev, spans, width, _ = band_ref.shape

    def one(q, carry):
        biases = [ext_scr[pl.ds(anchor + q + k, 1), :] for k in range(spans)]
        for start in range(0, width, CHUNK):
            total = jnp.zeros((CHUNK, width), F32)
            for k in range(spans):
                chunk = band_ref[q, k, start : start + CHUNK, :]
                if k == 0:
                    upper = rows_iota(chunk.shape) + start <= lanes_iota(chunk.shape)
                    chunk = jnp.where(upper, chunk, 0.0)
                total = total + chunk * biases[k]
            put_lane(racc_scr, start, anchor + q, jnp.sum(total, axis=1, keepdims=True))
        return carry

    lax.fori_loop(0, blk_dev, one, 0, unroll=True)


def trans_columns(trans_ref, info_ref, cols_scr, emit, ready):
    tiles, width, _ = trans_ref.shape

    def one(t, carry):
        ready(t)
        total = jnp.zeros((8, width), F32)
        for start in range(0, width, CHUNK):
            here = pick_lane(cols_scr, start, info_ref[8 + t])
            total = total + fold(trans_ref[t, start : start + CHUNK, :] * here)
        emit(t, jnp.sum(total, axis=0, keepdims=True))
        return carry

    lax.fori_loop(0, tiles, one, 0, unroll=True)


def trans_rows(trans_ref, info_ref, bias_of, racc_scr):
    tiles, width, _ = trans_ref.shape

    def one(t, carry):
        near, far = bias_of(t)
        for start in range(0, width, CHUNK):
            chunk = trans_ref[t, start : start + CHUNK, :]
            total = chunk[:, :LANES] * near + chunk[:, LANES:] * far
            put_lane(racc_scr, start, info_ref[8 + t], jnp.sum(total, axis=1, keepdims=True))
        return carry

    lax.fori_loop(0, tiles, one, 0, unroll=True)


def add_sums(code_of, half_of, steps, blk_g):
    out = [[jnp.zeros((8, LANES), F32) for _ in range(2)] for _ in range(blk_g)]
    for step in steps:
        code = code_of(step)
        for h in range(2):
            piece = half_of(step, h)
            for c in range(blk_g):
                out[c][h] = out[c][h] + jnp.where(code == c + 1.0, piece, 0.0)
    sums = [[jnp.sum(half, axis=0, keepdims=True) for half in pair] for pair in out]
    return jnp.concatenate([jnp.concatenate(pair, axis=1) for pair in sums], axis=0)


def nothing(_):
    pass


def quotient(value, size):
    if size & (size - 1):
        return lax.div(value, size)
    return lax.shift_right_logical(value, size.bit_length() - 1)


def fill_send(bias, info_ref, band_ref, trans_ref, send_ref, part_ref, scratch, band_ready,
              trans_ready):
    cols_scr, sums_scr, flat_scr, spill_scr = scratch
    blk_g = bias.shape[0]
    blk_dev, spans = band_ref.shape[:2]
    slot = 2 * blk_g
    half = slot // 2
    reach = spans - 1
    chip, core = lax.axis_index("chip"), lax.axis_index("core")
    here = 2 * chip + core
    for h in range(2):
        flat_scr[pl.ds(h, blk_g, stride=2), :] = bias[:, LANES * h : LANES * h + LANES]
    cols_scr[...] = columns_of(bias)
    flat = flat_scr[...]
    for at in range(send_ref.shape[0] // slot):
        send_ref[slot * at : slot * at + slot, :] = jnp.where(at < chip, flat, 0.0)

    def emit(t, sums):
        base = slot * quotient(info_ref[t], 2)
        odd = info_ref[t] & 1
        code = jnp.where(info_ref[t] == here, 0, info_ref[16 + t] + 1).astype(F32)
        for h in range(2):
            send_ref[pl.ds(base + 2 * odd + h, 1), :] = sums[:, LANES * h : LANES * h + LANES]
        send_ref[pl.ds(base + 4 + odd, 1), :] = jnp.full((1, LANES), code, F32)

    trans_columns(trans_ref, info_ref, cols_scr, emit, trans_ready)
    anchor = lax.axis_index("rep") * blk_dev
    band_columns(band_ref, cols_scr, sums_scr, anchor, band_ready)
    part_ref[...] = sums_scr[0:blk_g, :]
    for h in range(2):
        part = sums_scr[blk_g : blk_g + reach, LANES * h : LANES * h + LANES]
        spill_scr[pl.ds(h, reach, stride=2), :] = part
    spill = spill_scr[...]
    mine = pl.multiple_of(slot * chip, slot)
    send_ref[pl.ds(mine, half), :] = flat[0:half]
    send_ref[pl.ds(mine + half, half), :] = spill

    @pl.when((core == 1) & (chip < lax.axis_size("chip") - 1))
    def _():
        send_ref[pl.ds(mine + slot + half, half), :] = spill


def first_kernel(count_ref, masked_in, cols_in, rows_in, band_in, trans_in, own_ref, info_ref, send_ref,
                 part_ref, band_ref, trans_ref, masked_ref, cols_ref, rows_ref, sems, tile_sems,
                 flat_scr, *scratch):
    blk_g = own_ref.shape[0]
    blk_dev, tiles = band_ref.shape[0], trans_ref.shape[0]
    small = [
        pltpu.make_async_copy(src, dst, sems.at[i])
        for i, (src, dst) in enumerate(
            ((cols_in, cols_ref), (rows_in, rows_ref), (masked_in, masked_ref))
        )
    ]

    some = tiles // 2 if tiles % 2 == 0 else tiles

    def trans_copy(i):
        part = pl.ds(some * i, some)
        return pltpu.make_async_copy(trans_in.at[part], trans_ref.at[part], tile_sems.at[i])

    def band_copy(q):
        return pltpu.make_async_copy(band_in.at[q], band_ref.at[q], tile_sems.at[tiles + q])

    for copy in small:
        copy.start()
    for i in range(tiles // some):
        trans_copy(i).start(priority=i % 2)
    for q in range(blk_dev):
        band_copy(q).start(priority=q % 2)
    for copy in small:
        copy.wait()
    here = 2 * lax.axis_index("chip") + lax.axis_index("core")
    for t in range(tiles):
        used = t < count_ref[0]
        target = quotient(cols_ref[t], blk_g)
        info_ref[t] = jnp.where(used, target, here)
        info_ref[8 + t] = jnp.where(used, rows_ref[t] - here * blk_g, LANES - 1)
        info_ref[16 + t] = cols_ref[t] - target * blk_g
    flat_scr[...] = 1.0 - masked_ref[...].astype(F32)
    own = jnp.concatenate([flat_scr[pl.ds(h, blk_g, stride=2), :] for h in range(2)], axis=1)
    own_ref[...] = own

    def trans_ready(t):
        @pl.when(t % some == 0)
        def _():
            trans_copy(t // some).wait()

    fill_send(own, info_ref, band_ref, trans_ref, send_ref, part_ref, scratch,
              lambda q: band_copy(q).wait(), trans_ready)


def spread(value, scr):
    scr[...] = value
    n = value.shape[0] // 2
    return jnp.concatenate([scr[pl.ds(h, n, stride=2), :] for h in range(2)], axis=1)


def meet_kernel(own_ref, part_ref, got_ref, mate_ref, info_in, band_ref, trans_ref,
                share_ref, code_ref, info_ref, info_sem, ext_scr, racc_scr, near_scr):
    table = pltpu.make_async_copy(info_in, info_ref, info_sem)
    table.start()
    blk_g, width = own_ref.shape
    blk_dev, spans = band_ref.shape[:2]
    reach = spans - 1
    slot = 2 * blk_g
    half = slot // 2
    chips = got_ref.shape[0] // slot
    chip, core = lax.axis_index("chip"), lax.axis_index("core")
    anchor = lax.axis_index("rep") * blk_dev
    first = core == 0
    at = pl.multiple_of(slot * jnp.minimum(chip + core, chips - 1), slot)
    ahead = jnp.where(chip + core < chips, mate_ref[pl.ds(at, half), :], 0.0)
    at = pl.multiple_of(slot * jnp.maximum(chip + core - 1, 0), slot)
    back = jnp.where(chip + core > 0, mate_ref[pl.ds(at + half, half), :], 0.0)
    ext_scr[0:blk_g, :] = own_ref[...]
    ext_scr[blk_g : blk_g + reach, :] = spread(ahead, near_scr)
    racc_scr[...] = jnp.zeros(racc_scr.shape, F32)
    band_rows(band_ref, ext_scr, racc_scr, anchor)
    table.wait()

    def bias_of(t):
        source = info_ref[t]
        row = slot * quotient(source, 2) + 2 * info_ref[16 + t]
        same = (source & 1) == core
        return [
            jnp.where(same, got_ref[pl.ds(row + h, 1), :], mate_ref[pl.ds(row + h, 1), :])
            for h in range(2)
        ]

    trans_rows(trans_ref, info_ref, bias_of, racc_scr)

    def pick(ref, step, row):
        even, odd = row
        base = step * 8 * slot
        return jnp.where(
            first,
            ref[pl.ds(base + even, 8, stride=slot), :],
            ref[pl.ds(base + odd, 8, stride=slot), :],
        )

    steps = [(i, step) for i in range(2) for step in range(chips // 8)]
    refs = (got_ref, mate_ref)

    def code_of(which):
        i, step = which
        code = pick(refs[i], step, (4, 5))
        return jnp.where(rows_iota(code.shape) + 8 * step < chip, code, 0.0)

    sums = add_sums(code_of, lambda w, h: pick(refs[w[0]], w[1], (h, 2 + h)), steps, blk_g)
    for i in range(2):
        code = got_ref[pl.ds(4 + i, chips, stride=slot), :]
        code_ref[i] = jnp.where(rows_iota(code.shape) < chip, code, 0.0)
    total = part_ref[...] + jnp.transpose(racc_scr[...])[0:blk_g, :] + sums
    total = total + jnp.concatenate(
        [spread(back, near_scr), jnp.zeros((blk_g - reach, width), F32)], axis=0
    )
    total = jnp.where(own_ref[...] > 0.0, total, jnp.inf)
    for s in range(share_ref.shape[0]):
        share_ref[s] = total


def halves(block):
    return [block[:, LANES * h : LANES * h + LANES] for h in range(2)]


def whole_sum(block):
    return jnp.sum(jnp.sum(block, axis=0, keepdims=True), axis=1, keepdims=True)


def in_lanes(shape, *values):
    lane = lanes_iota(shape)
    out = jnp.zeros(shape, F32)
    for i, value in enumerate(values):
        out = jnp.where(lane == i, value, out)
    return out


def lane_of(block, at):
    return jnp.sum(jnp.where(lanes_iota(block.shape) == at, block, 0.0), axis=1, keepdims=True)


def second_kernel(shares_ref, code_ref, info_in, band_ref, trans_ref, ext_ref, first_ref, send_ref,
                  part_ref, info_ref, info_sem, cols_scr, sums_scr, spill_scr, ahead_scr):
    table = pltpu.make_async_copy(info_in, info_ref, info_sem)
    table.start()
    blk_g = shares_ref.shape[1]
    blk_dev, spans = band_ref.shape[:2]
    reach = spans - 1
    replicas = shares_ref.shape[0] // 2
    chips = send_ref.shape[0] // STEP
    chip, core = lax.axis_index("chip"), lax.axis_index("core")
    first = core == 0
    biases, sums, counts = [], [], []
    for c in range(2):
        total = shares_ref[c * replicas]
        for s in range(1, replicas):
            total = total + shares_ref[c * replicas + s]
        kept = total != jnp.inf
        sums.append(jnp.where(kept, total, 0.0))
        counts.append(jnp.where(kept, 1.0, 0.0))
        biases.append(jnp.where(kept, 1.0 / jnp.where(kept, total, 1.0), 0.0))
    sum_one, count = whole_sum(sums[0] + sums[1]), whole_sum(counts[0] + counts[1])
    scale = sum_one / jnp.maximum(count, 1.0)
    scale = jnp.where(scale == 0.0, 1.0, scale)
    first_ref[...] = in_lanes(first_ref.shape, sum_one, 0.0, scale, count)
    own = jnp.where(first, biases[0], biases[1])
    ext_ref[0:blk_g, :] = own
    ext_ref[blk_g:, :] = jnp.where(first, biases[1], biases[0])
    cols_scr[...] = columns_of(own)
    for i in range(2):
        pieces = halves(biases[i])
        for at in range(0, chips, 8):
            code = code_ref[i, at : at + 8, :]
            for h in range(2):
                piece = jnp.zeros((8, LANES), F32)
                for c in range(blk_g):
                    piece = jnp.where(code == c + 1.0, pieces[h][c : c + 1], piece)
                send_ref[pl.ds(STEP * at + 2 - 2 * i + h, 8, stride=STEP), :] = piece

    def emit(t, sums):
        base = STEP * quotient(info_ref[t], 2) + 2 - 2 * (info_ref[t] & 1)
        for h in range(2):
            send_ref[pl.ds(base + h, 1), :] = halves(sums)[h]

    band_columns(band_ref, cols_scr, sums_scr, lax.axis_index("rep") * blk_dev, nothing)
    table.wait()
    trans_columns(trans_ref, info_ref, cols_scr, emit, nothing)
    spill = sums_scr[blk_g : blk_g + reach, :]
    part_ref[0:blk_g, :] = sums_scr[0:blk_g, :]
    mate = jnp.concatenate([spill, jnp.zeros((blk_g - reach, own.shape[1]), F32)], axis=0)
    part_ref[blk_g : 2 * blk_g, :] = jnp.where(first, mate, 0.0)
    for h in range(2):
        spill_scr[pl.ds(h, reach, stride=2), :] = halves(spill)[h]
        ahead_scr[pl.ds(h, reach, stride=2), :] = halves(biases[0])[h][0:reach]

    @pl.when((core == 1) & (chip > 0))
    def _():
        for i in range(2 * reach):
            send_ref[pl.ds(STEP * (chip - 1) + 2 + i, 1), :] = ahead_scr[i : i + 1, :]

    @pl.when((core == 1) & (chip < chips - 1))
    def _():
        for i in range(2 * reach):
            send_ref[pl.ds(STEP * (chip + 1) + 2 + i, 1), :] = spill_scr[i : i + 1, :]


def third_kernel(code_ref, got_ref, ext_ref, part_ref, first_ref, info_in, band_ref, trans_ref, share_ref,
                 info_ref, info_sem, ext_scr, racc_scr, near_scr):
    table = pltpu.make_async_copy(info_in, info_ref, info_sem)
    table.start()
    blk_g = part_ref.shape[0] // 2
    blk_dev, spans = band_ref.shape[:2]
    reach = spans - 1
    replicas = share_ref.shape[0] // (2 * SHARE)
    chips = got_ref.shape[0] // STEP
    chip, core = lax.axis_index("chip"), lax.axis_index("core")
    first = core == 0
    ext_scr[...] = ext_ref[...]
    racc_scr[...] = jnp.zeros(racc_scr.shape, F32)

    def edge(at, valid):
        at = jnp.clip(at, 0, chips - 1)
        for i in range(2 * reach):
            near_scr[i : i + 1, :] = got_ref[pl.ds(STEP * at + 2 + i, 1), :]
        block = jnp.concatenate([near_scr[pl.ds(h, reach, stride=2), :] for h in range(2)], axis=1)
        return jnp.where(valid, block, 0.0)

    ahead = edge(chip + 1, chip + 1 < chips)
    ext_scr[blk_g : blk_g + reach, :] = jnp.where(first, ext_ref[blk_g : blk_g + reach, :], ahead)
    back = edge(chip - 1, (core == 1) & (chip > 0))
    band_rows(band_ref, ext_scr, racc_scr, lax.axis_index("rep") * blk_dev)
    table.wait()

    def bias_of(t):
        base = STEP * quotient(info_ref[t], 2) + 2 - 2 * (info_ref[t] & 1)
        return [got_ref[pl.ds(base + h, 1), :] for h in range(2)]

    trans_rows(trans_ref, info_ref, bias_of, racc_scr)
    sums = [
        add_sums(
            lambda at: code_ref[i, at : at + 8, :],
            lambda at, h: got_ref[pl.ds(STEP * at + 2 - 2 * i + h, 8, stride=STEP), :],
            range(0, chips, 8),
            blk_g,
        )
        for i in range(2)
    ]
    own = part_ref[0:blk_g, :] + jnp.transpose(racc_scr[...])[0:blk_g, :]
    own = own + jnp.where(first, sums[0], sums[1])
    mate = part_ref[blk_g : 2 * blk_g, :] + jnp.where(first, sums[1], sums[0])
    mate = mate + jnp.concatenate([back, jnp.zeros((blk_g - reach, own.shape[1]), F32)], axis=0)
    scale = lane_of(first_ref[0:1, :], 2)
    weighed = (ext_ref[0:blk_g, :] * scale) * (own * scale)
    sum_two = whole_sum(weighed + (ext_ref[blk_g:, :] * scale) * (mate * scale))
    for c in range(2):
        pieces = halves(jnp.where(core == c, own, mate))
        for s in range(replicas):
            at = SHARE * (c * replicas + s)
            for h in range(2):
                share_ref[pl.ds(at + h, blk_g, stride=2), :] = pieces[h]
            share_ref[at + 2 * blk_g : at + SHARE, :] = jnp.broadcast_to(sum_two, (2, LANES))


def stats_kernel(shares_ref, first_ref, second_ref, stats_ref):
    size = SHARE - 2
    shares = [shares_ref[at : at + SHARE, :] for at in range(0, shares_ref.shape[0], SHARE)]
    total = shares[0]
    for share in shares[1:]:
        total = total + share
    second_ref[...] = total[0:size]
    stats = jnp.where(lanes_iota((1, LANES)) == 1, total[size : size + 1], first_ref[0:1, :])
    stats_ref[...] = jnp.broadcast_to(stats, stats_ref.shape)


def final_kernel(stats_ref, own_ref, ext_ref, second_ref, weights_ref, coverage_ref):
    stats = stats_ref[...]
    count = jnp.sum(lane_of(stats, 3), axis=0, keepdims=True)
    average_one = jnp.sum(lane_of(stats, 0), axis=0, keepdims=True) / count
    ratio = average_one / lane_of(stats, 2)
    average_two = jnp.sum(lane_of(stats, 1) * ratio * ratio, axis=0, keepdims=True) / count
    blk_g = own_ref.shape[0]
    owns, biases = halves(own_ref[...]), halves(ext_ref[0:blk_g, :])
    for h in range(2):
        rows = pl.ds(h, blk_g, stride=2)
        kept = owns[h] > 0.0
        total = second_ref[rows, :] * average_one
        coverage_ref[rows, :] = (biases[h] * average_one) * total
        weights_ref[rows, :] = jnp.where(kept, average_two / jnp.where(kept, total, 1.0), 0.0)


def call(kernel, ins, outs, scratch=(), cost=None, limit=16):
    return pl.pallas_call(
        kernel,
        in_specs=list(ins),
        out_shape=[jax.ShapeDtypeStruct(s, d) for s, d, _ in outs],
        out_specs=[spec for _, _, spec in outs],
        scratch_shapes=list(scratch),
        compiler_params=pltpu.CompilerParams(vmem_limit_bytes=limit * 1024 * 1024),
        cost_estimate=cost and pl.CostEstimate(flops=cost, bytes_accessed=cost, transcendentals=0),
    )


def floats(*shape):
    return (shape, F32, VMEM)


def exchange(block, axis):
    return lax.all_to_all(block, axis, 0, 0, tiled=True)


def swap_cores(block):
    return lax.ppermute(block, "core", [(0, 1), (1, 0)])


def shards(band, trans, rows_at, cols_at, trans_count, masked):
    blk_dev, spans, width, _ = band.shape
    tiles = trans.shape[0]
    replicas = lax.axis_size("rep")
    chips = lax.axis_size("chip")
    blk_g = blk_dev * replicas
    own_like = floats(blk_g, width)
    send_like = floats(chips * 2 * blk_g, LANES)
    share_like = floats(2 * replicas, blk_g, width)
    cols_scr = pltpu.VMEM((width, LANES), F32)
    wide_scr = pltpu.VMEM((16, width), F32)
    flat_scr = pltpu.VMEM((2 * blk_g, LANES), F32)
    half_scr = pltpu.VMEM((2 * spans - 2, LANES), F32)
    info_scr = [pltpu.SMEM((24,), I32), pltpu.SemaphoreType.DMA(())]
    fill_scr = [cols_scr, wide_scr, flat_scr, half_scr]
    masked, cols_at, rows_at, band, trans = (
        pltpu.with_memory_space_constraint(x, pltpu.HBM)
        for x in (masked.reshape(2 * blk_g, LANES), cols_at, rows_at, band, trans)
    )
    own, info, send, part, band, trans = pl.pallas_call(
        first_kernel,
        in_specs=[SMEM] + [HBM] * 5,
        out_shape=[
            jax.ShapeDtypeStruct((blk_g, width), F32),
            jax.ShapeDtypeStruct((24,), I32),
            jax.ShapeDtypeStruct((chips * 2 * blk_g, LANES), F32),
            jax.ShapeDtypeStruct((blk_g, width), F32),
            pltpu.VMEM(band.shape, F32),
            pltpu.VMEM(trans.shape, F32),
        ],
        out_specs=[VMEM, SMEM, VMEM, VMEM, VMEM, VMEM],
        scratch_shapes=[
            pltpu.VMEM((2 * blk_g, LANES), I32),
            pltpu.SMEM((tiles,), I32),
            pltpu.SMEM((tiles,), I32),
            pltpu.SemaphoreType.DMA((3,)),
            pltpu.SemaphoreType.DMA((tiles + blk_dev,)),
            flat_scr,
        ] + fill_scr,
        compiler_params=pltpu.CompilerParams(vmem_limit_bytes=16 * 1024 * 1024),
    )(trans_count, masked, cols_at, rows_at, band, trans)
    got = exchange(send.reshape(chips, 1, 2 * blk_g * LANES), "chip").reshape(send.shape)
    mate = swap_cores(got)
    share, code = call(
        meet_kernel,
        [VMEM, VMEM, VMEM, VMEM, ANY, VMEM, VMEM],
        [share_like, floats(2, chips, LANES)],
        info_scr + [wide_scr, cols_scr, half_scr],
    )(own, part, got, mate, info, band, trans)
    shares = exchange(share, LOCAL)
    ext, first, send, part = call(
        second_kernel,
        [VMEM, VMEM, ANY, VMEM, VMEM],
        [floats(2 * blk_g, width), floats(8, LANES), floats(STEP * chips, LANES),
         floats(2 * blk_g, width)],
        info_scr + [cols_scr, wide_scr, half_scr, half_scr],
    )(shares, code, info, band, trans)
    got = exchange(send.reshape(STEP * chips // 2, 2, LANES), "chip").reshape(send.shape)
    (share,) = call(
        third_kernel,
        [VMEM, VMEM, VMEM, VMEM, VMEM, ANY, VMEM, VMEM],
        [floats(2 * replicas * SHARE, LANES)],
        info_scr + [wide_scr, cols_scr, half_scr],
    )(code, got, ext, part, first, info, band, trans)
    shares = exchange(share.reshape(replicas * SHARE, 2, LANES), LOCAL).reshape(share.shape)
    second, stats = call(
        stats_kernel, [VMEM, VMEM], [floats(2 * blk_g, LANES), floats(chips, LANES)]
    )(shares, first)
    stats = exchange(stats, "chip")
    weights, coverage = call(
        final_kernel, [VMEM] * 4, [floats(2 * blk_g, LANES)] * 2
    )(stats, own, ext, second)
    return (weights.reshape(-1), coverage.reshape(-1))


GENOME = ("chip", "core")
LOCAL = ("core", "rep")
STEP = 10
SHARE = 18


def solution(mesh):
    names = mesh.axis_names
    groups, replicas = (mesh.shape[name] for name in ("genome", "rep"))
    assert names == ("genome", "rep")
    devices = mesh.devices.reshape(groups // 2, 2, replicas)
    split = Mesh(devices, GENOME + ("rep",))
    every = P(GENOME + ("rep",))
    out_specs = (P(GENOME), P(GENOME))
    return jax.shard_map(
        shards, mesh=split, in_specs=(every,) * 5 + (P(GENOME),), out_specs=out_specs, check_vma=False
    )
```

```python
import functools

import jax
import jax.numpy as jnp
from jax import lax
from jax.experimental import pallas as pl
from jax.experimental.pallas import tpu as pltpu
from jax.sharding import Mesh, PartitionSpec as P

F32 = jnp.float32
I32 = jnp.int32
LANES = 128
CHUNK = 32
VMEM = pl.BlockSpec(memory_space=pltpu.VMEM)
SMEM = pl.BlockSpec(memory_space=pltpu.SMEM)
HBM = pl.BlockSpec(memory_space=pltpu.HBM)
ANY = pl.BlockSpec(memory_space=pl.ANY)


def rows_iota(shape):
    return lax.broadcasted_iota(I32, shape, 0)


def lanes_iota(shape):
    return lax.broadcasted_iota(I32, shape, 1)


def columns_of(block_rows):
    n, width = block_rows.shape
    padded = jnp.concatenate([block_rows, jnp.zeros((LANES - n, width), F32)], axis=0)
    return jnp.transpose(padded)


def pick_lane(ref, start, lane):
    chunk = ref[start : start + CHUNK, :]
    return jnp.sum(jnp.where(lanes_iota(chunk.shape) == lane, chunk, 0.0), axis=1, keepdims=True)


def fold(chunk):
    total = chunk[0:8]
    for at in range(8, chunk.shape[0], 8):
        total = total + chunk[at : at + 8]
    return total


def put_lane(ref, start, lane, column):
    hit = lanes_iota((CHUNK, LANES)) == lane
    ref[start : start + CHUNK, :] += jnp.where(hit, column, 0.0)


def band_columns(band_ref, cols_scr, sums_scr, anchor, ready):
    blk_dev, spans, width, _ = band_ref.shape
    sums_scr[...] = jnp.zeros(sums_scr.shape, F32)

    def one(q, carry):
        ready(q)
        sums = [jnp.zeros((8, width), F32) for _ in range(spans)]
        for start in range(0, width, CHUNK):
            here = pick_lane(cols_scr, start, anchor + q)
            for k in range(spans):
                chunk = band_ref[q, k, start : start + CHUNK, :]
                if k == 0:
                    above = rows_iota(chunk.shape) + start < lanes_iota(chunk.shape)
                    chunk = jnp.where(above, chunk, 0.0)
                sums[k] = sums[k] + fold(chunk * here)
        for k in range(spans):
            sums_scr[pl.ds(anchor + q + k, 1), :] += jnp.sum(sums[k], axis=0, keepdims=True)
        return carry

    lax.fori_loop(0, blk_dev, one, 0, unroll=True)


def band_rows(band_ref, ext_scr, racc_scr, anchor):
    blk_dev, spans, width, _ = band_ref.shape

    def one(q, carry):
        biases = [ext_scr[pl.ds(anchor + q + k, 1), :] for k in range(spans)]
        for start in range(0, width, CHUNK):
            total = jnp.zeros((CHUNK, width), F32)
            for k in range(spans):
                chunk = band_ref[q, k, start : start + CHUNK, :]
                if k == 0:
                    upper = rows_iota(chunk.shape) + start <= lanes_iota(chunk.shape)
                    chunk = jnp.where(upper, chunk, 0.0)
                total = total + chunk * biases[k]
            put_lane(racc_scr, start, anchor + q, jnp.sum(total, axis=1, keepdims=True))
        return carry

    lax.fori_loop(0, blk_dev, one, 0, unroll=True)


def trans_columns(trans_ref, info_ref, cols_scr, emit, ready):
    tiles, width, _ = trans_ref.shape

    def one(t, carry):
        ready(t)
        total = jnp.zeros((8, width), F32)
        for start in range(0, width, CHUNK):
            here = pick_lane(cols_scr, start, info_ref[8 + t])
            total = total + fold(trans_ref[t, start : start + CHUNK, :] * here)
        emit(t, jnp.sum(total, axis=0, keepdims=True))
        return carry

    lax.fori_loop(0, tiles, one, 0, unroll=True)


def trans_rows(trans_ref, info_ref, bias_of, racc_scr):
    tiles, width, _ = trans_ref.shape

    def one(t, carry):
        near, far = bias_of(t)
        for start in range(0, width, CHUNK):
            chunk = trans_ref[t, start : start + CHUNK, :]
            total = chunk[:, :LANES] * near + chunk[:, LANES:] * far
            put_lane(racc_scr, start, info_ref[8 + t], jnp.sum(total, axis=1, keepdims=True))
        return carry

    lax.fori_loop(0, tiles, one, 0, unroll=True)


def add_sums(code_of, half_of, steps, blk_g):
    out = [[jnp.zeros((8, LANES), F32) for _ in range(2)] for _ in range(blk_g)]
    for step in steps:
        code = code_of(step)
        for h in range(2):
            piece = half_of(step, h)
            for c in range(blk_g):
                out[c][h] = out[c][h] + jnp.where(code == c + 1.0, piece, 0.0)
    sums = [[jnp.sum(half, axis=0, keepdims=True) for half in pair] for pair in out]
    return jnp.concatenate([jnp.concatenate(pair, axis=1) for pair in sums], axis=0)


def nothing(_):
    pass


def quotient(value, size):
    if size & (size - 1):
        return lax.div(value, size)
    return lax.shift_right_logical(value, size.bit_length() - 1)


def fill_send(bias, info_ref, band_ref, trans_ref, send_ref, part_ref, scratch, band_ready,
              trans_ready):
    cols_scr, sums_scr, flat_scr, spill_scr = scratch
    blk_g = bias.shape[0]
    blk_dev, spans = band_ref.shape[:2]
    slot = 2 * blk_g
    half = slot // 2
    reach = spans - 1
    chip, core = lax.axis_index("chip"), lax.axis_index("core")
    here = 2 * chip + core
    for h in range(2):
        flat_scr[pl.ds(h, blk_g, stride=2), :] = bias[:, LANES * h : LANES * h + LANES]
    cols_scr[...] = columns_of(bias)
    flat = flat_scr[...]
    for at in range(send_ref.shape[0] // slot):
        send_ref[slot * at : slot * at + slot, :] = jnp.where(at < chip, flat, 0.0)

    def emit(t, sums):
        base = slot * quotient(info_ref[t], 2)
        odd = info_ref[t] & 1
        code = jnp.where(info_ref[t] == here, 0, info_ref[16 + t] + 1).astype(F32)
        for h in range(2):
            send_ref[pl.ds(base + 2 * odd + h, 1), :] = sums[:, LANES * h : LANES * h + LANES]
        send_ref[pl.ds(base + 4 + odd, 1), :] = jnp.full((1, LANES), code, F32)

    trans_columns(trans_ref, info_ref, cols_scr, emit, trans_ready)
    anchor = lax.axis_index("rep") * blk_dev
    band_columns(band_ref, cols_scr, sums_scr, anchor, band_ready)
    part_ref[...] = sums_scr[0:blk_g, :]
    for h in range(2):
        part = sums_scr[blk_g : blk_g + reach, LANES * h : LANES * h + LANES]
        spill_scr[pl.ds(h, reach, stride=2), :] = part
    spill = spill_scr[...]
    mine = pl.multiple_of(slot * chip, slot)
    send_ref[pl.ds(mine, half), :] = flat[0:half]
    send_ref[pl.ds(mine + half, half), :] = spill

    @pl.when((core == 1) & (chip < lax.axis_size("chip") - 1))
    def _():
        send_ref[pl.ds(mine + slot + half, half), :] = spill


def first_kernel(count_ref, masked_in, cols_in, rows_in, band_in, trans_in, own_ref, info_ref, send_ref,
                 part_ref, band_ref, trans_ref, masked_ref, cols_ref, rows_ref, sems, tile_sems,
                 flat_scr, *scratch):
    blk_g = own_ref.shape[0]
    blk_dev, tiles = band_ref.shape[0], trans_ref.shape[0]
    small = [
        pltpu.make_async_copy(src, dst, sems.at[i])
        for i, (src, dst) in enumerate(
            ((cols_in, cols_ref), (rows_in, rows_ref), (masked_in, masked_ref))
        )
    ]

    some = tiles // 2 if tiles % 2 == 0 else tiles

    def trans_copy(i):
        part = pl.ds(some * i, some)
        return pltpu.make_async_copy(trans_in.at[part], trans_ref.at[part], tile_sems.at[i])

    def band_copy(q):
        return pltpu.make_async_copy(band_in.at[q], band_ref.at[q], tile_sems.at[tiles + q])

    for copy in small:
        copy.start()
    for i in range(tiles // some):
        trans_copy(i).start(priority=i % 2)
    for q in range(blk_dev):
        band_copy(q).start(priority=q % 2)
    for copy in small:
        copy.wait()
    here = 2 * lax.axis_index("chip") + lax.axis_index("core")
    for t in range(tiles):
        used = t < count_ref[0]
        target = quotient(cols_ref[t], blk_g)
        info_ref[t] = jnp.where(used, target, here)
        info_ref[8 + t] = jnp.where(used, rows_ref[t] - here * blk_g, LANES - 1)
        info_ref[16 + t] = cols_ref[t] - target * blk_g
    flat_scr[...] = 1.0 - masked_ref[...].astype(F32)
    own = jnp.concatenate([flat_scr[pl.ds(h, blk_g, stride=2), :] for h in range(2)], axis=1)
    own_ref[...] = own

    def trans_ready(t):
        @pl.when(t % some == 0)
        def _():
            trans_copy(t // some).wait()

    fill_send(own, info_ref, band_ref, trans_ref, send_ref, part_ref, scratch,
              lambda q: band_copy(q).wait(), trans_ready)


def spread(value, scr):
    scr[...] = value
    n = value.shape[0] // 2
    return jnp.concatenate([scr[pl.ds(h, n, stride=2), :] for h in range(2)], axis=1)


def meet_kernel(own_ref, part_ref, got_ref, mate_ref, info_in, band_ref, trans_ref,
                share_ref, code_ref, info_ref, info_sem, ext_scr, racc_scr, near_scr):
    table = pltpu.make_async_copy(info_in, info_ref, info_sem)
    table.start()
    blk_g, width = own_ref.shape
    blk_dev, spans = band_ref.shape[:2]
    reach = spans - 1
    slot = 2 * blk_g
    half = slot // 2
    chips = got_ref.shape[0] // slot
    chip, core = lax.axis_index("chip"), lax.axis_index("core")
    anchor = lax.axis_index("rep") * blk_dev
    first = core == 0
    at = pl.multiple_of(slot * jnp.minimum(chip + core, chips - 1), slot)
    ahead = jnp.where(chip + core < chips, mate_ref[pl.ds(at, half), :], 0.0)
    at = pl.multiple_of(slot * jnp.maximum(chip + core - 1, 0), slot)
    back = jnp.where(chip + core > 0, mate_ref[pl.ds(at + half, half), :], 0.0)
    ext_scr[0:blk_g, :] = own_ref[...]
    ext_scr[blk_g : blk_g + reach, :] = spread(ahead, near_scr)
    racc_scr[...] = jnp.zeros(racc_scr.shape, F32)
    band_rows(band_ref, ext_scr, racc_scr, anchor)
    table.wait()

    def bias_of(t):
        source = info_ref[t]
        row = slot * quotient(source, 2) + 2 * info_ref[16 + t]
        same = (source & 1) == core
        return [
            jnp.where(same, got_ref[pl.ds(row + h, 1), :], mate_ref[pl.ds(row + h, 1), :])
            for h in range(2)
        ]

    trans_rows(trans_ref, info_ref, bias_of, racc_scr)

    def pick(ref, step, row):
        even, odd = row
        base = step * 8 * slot
        return jnp.where(
            first,
            ref[pl.ds(base + even, 8, stride=slot), :],
            ref[pl.ds(base + odd, 8, stride=slot), :],
        )

    steps = [(i, step) for i in range(2) for step in range(chips // 8)]
    refs = (got_ref, mate_ref)

    def code_of(which):
        i, step = which
        code = pick(refs[i], step, (4, 5))
        return jnp.where(rows_iota(code.shape) + 8 * step < chip, code, 0.0)

    sums = add_sums(code_of, lambda w, h: pick(refs[w[0]], w[1], (h, 2 + h)), steps, blk_g)
    for i in range(2):
        code = got_ref[pl.ds(4 + i, chips, stride=slot), :]
        code_ref[i] = jnp.where(rows_iota(code.shape) < chip, code, 0.0)
    total = part_ref[...] + jnp.transpose(racc_scr[...])[0:blk_g, :] + sums
    total = total + jnp.concatenate(
        [spread(back, near_scr), jnp.zeros((blk_g - reach, width), F32)], axis=0
    )
    total = jnp.where(own_ref[...] > 0.0, total, jnp.inf)
    for s in range(share_ref.shape[0]):
        share_ref[s] = total


def halves(block):
    return [block[:, LANES * h : LANES * h + LANES] for h in range(2)]


def whole_sum(block):
    return jnp.sum(jnp.sum(block, axis=0, keepdims=True), axis=1, keepdims=True)


def in_lanes(shape, *values):
    lane = lanes_iota(shape)
    out = jnp.zeros(shape, F32)
    for i, value in enumerate(values):
        out = jnp.where(lane == i, value, out)
    return out


def lane_of(block, at):
    return jnp.sum(jnp.where(lanes_iota(block.shape) == at, block, 0.0), axis=1, keepdims=True)


def second_kernel(shares_ref, code_ref, info_in, band_ref, trans_ref, ext_ref, first_ref, send_ref,
                  part_ref, info_ref, info_sem, cols_scr, sums_scr, spill_scr, ahead_scr):
    table = pltpu.make_async_copy(info_in, info_ref, info_sem)
    table.start()
    blk_g = shares_ref.shape[1]
    blk_dev, spans = band_ref.shape[:2]
    reach = spans - 1
    replicas = shares_ref.shape[0] // 2
    chips = send_ref.shape[0] // STEP
    chip, core = lax.axis_index("chip"), lax.axis_index("core")
    first = core == 0
    biases, sums, counts = [], [], []
    for c in range(2):
        total = shares_ref[c * replicas]
        for s in range(1, replicas):
            total = total + shares_ref[c * replicas + s]
        kept = total != jnp.inf
        sums.append(jnp.where(kept, total, 0.0))
        counts.append(jnp.where(kept, 1.0, 0.0))
        biases.append(jnp.where(kept, 1.0 / jnp.where(kept, total, 1.0), 0.0))
    sum_one, count = whole_sum(sums[0] + sums[1]), whole_sum(counts[0] + counts[1])
    scale = sum_one / jnp.maximum(count, 1.0)
    scale = jnp.where(scale == 0.0, 1.0, scale)
    first_ref[...] = in_lanes(first_ref.shape, sum_one, 0.0, scale, count)
    own = jnp.where(first, biases[0], biases[1])
    ext_ref[0:blk_g, :] = own
    ext_ref[blk_g:, :] = jnp.where(first, biases[1], biases[0])
    cols_scr[...] = columns_of(own)
    for i in range(2):
        pieces = halves(biases[i])
        for at in range(0, chips, 8):
            code = code_ref[i, at : at + 8, :]
            for h in range(2):
                piece = jnp.zeros((8, LANES), F32)
                for c in range(blk_g):
                    piece = jnp.where(code == c + 1.0, pieces[h][c : c + 1], piece)
                send_ref[pl.ds(STEP * at + 2 - 2 * i + h, 8, stride=STEP), :] = piece

    def emit(t, sums):
        base = STEP * quotient(info_ref[t], 2) + 2 - 2 * (info_ref[t] & 1)
        for h in range(2):
            send_ref[pl.ds(base + h, 1), :] = halves(sums)[h]

    band_columns(band_ref, cols_scr, sums_scr, lax.axis_index("rep") * blk_dev, nothing)
    table.wait()
    trans_columns(trans_ref, info_ref, cols_scr, emit, nothing)
    spill = sums_scr[blk_g : blk_g + reach, :]
    part_ref[0:blk_g, :] = sums_scr[0:blk_g, :]
    mate = jnp.concatenate([spill, jnp.zeros((blk_g - reach, own.shape[1]), F32)], axis=0)
    part_ref[blk_g : 2 * blk_g, :] = jnp.where(first, mate, 0.0)
    for h in range(2):
        spill_scr[pl.ds(h, reach, stride=2), :] = halves(spill)[h]
        ahead_scr[pl.ds(h, reach, stride=2), :] = halves(biases[0])[h][0:reach]

    @pl.when((core == 1) & (chip > 0))
    def _():
        for i in range(2 * reach):
            send_ref[pl.ds(STEP * (chip - 1) + 2 + i, 1), :] = ahead_scr[i : i + 1, :]

    @pl.when((core == 1) & (chip < chips - 1))
    def _():
        for i in range(2 * reach):
            send_ref[pl.ds(STEP * (chip + 1) + 2 + i, 1), :] = spill_scr[i : i + 1, :]


def third_kernel(code_ref, got_ref, ext_ref, part_ref, first_ref, info_in, band_ref, trans_ref, share_ref,
                 info_ref, info_sem, ext_scr, racc_scr, near_scr):
    table = pltpu.make_async_copy(info_in, info_ref, info_sem)
    table.start()
    blk_g = part_ref.shape[0] // 2
    blk_dev, spans = band_ref.shape[:2]
    reach = spans - 1
    replicas = share_ref.shape[0] // (2 * SHARE)
    chips = got_ref.shape[0] // STEP
    chip, core = lax.axis_index("chip"), lax.axis_index("core")
    first = core == 0
    ext_scr[...] = ext_ref[...]
    racc_scr[...] = jnp.zeros(racc_scr.shape, F32)

    def edge(at, valid):
        at = jnp.clip(at, 0, chips - 1)
        for i in range(2 * reach):
            near_scr[i : i + 1, :] = got_ref[pl.ds(STEP * at + 2 + i, 1), :]
        block = jnp.concatenate([near_scr[pl.ds(h, reach, stride=2), :] for h in range(2)], axis=1)
        return jnp.where(valid, block, 0.0)

    ahead = edge(chip + 1, chip + 1 < chips)
    ext_scr[blk_g : blk_g + reach, :] = jnp.where(first, ext_ref[blk_g : blk_g + reach, :], ahead)
    back = edge(chip - 1, (core == 1) & (chip > 0))
    band_rows(band_ref, ext_scr, racc_scr, lax.axis_index("rep") * blk_dev)
    table.wait()

    def bias_of(t):
        base = STEP * quotient(info_ref[t], 2) + 2 - 2 * (info_ref[t] & 1)
        return [got_ref[pl.ds(base + h, 1), :] for h in range(2)]

    trans_rows(trans_ref, info_ref, bias_of, racc_scr)
    sums = [
        add_sums(
            lambda at: code_ref[i, at : at + 8, :],
            lambda at, h: got_ref[pl.ds(STEP * at + 2 - 2 * i + h, 8, stride=STEP), :],
            range(0, chips, 8),
            blk_g,
        )
        for i in range(2)
    ]
    own = part_ref[0:blk_g, :] + jnp.transpose(racc_scr[...])[0:blk_g, :]
    own = own + jnp.where(first, sums[0], sums[1])
    mate = part_ref[blk_g : 2 * blk_g, :] + jnp.where(first, sums[1], sums[0])
    mate = mate + jnp.concatenate([back, jnp.zeros((blk_g - reach, own.shape[1]), F32)], axis=0)
    scale = lane_of(first_ref[0:1, :], 2)
    weighed = (ext_ref[0:blk_g, :] * scale) * (own * scale)
    sum_two = whole_sum(weighed + (ext_ref[blk_g:, :] * scale) * (mate * scale))
    for c in range(2):
        pieces = halves(jnp.where(core == c, own, mate))
        for s in range(replicas):
            at = SHARE * (c * replicas + s)
            for h in range(2):
                share_ref[pl.ds(at + h, blk_g, stride=2), :] = pieces[h]
            share_ref[at + 2 * blk_g : at + SHARE, :] = jnp.broadcast_to(sum_two, (2, LANES))


def stats_kernel(shares_ref, first_ref, second_ref, stats_ref):
    size = SHARE - 2
    shares = [shares_ref[at : at + SHARE, :] for at in range(0, shares_ref.shape[0], SHARE)]
    total = shares[0]
    for share in shares[1:]:
        total = total + share
    second_ref[...] = total[0:size]
    stats = jnp.where(lanes_iota((1, LANES)) == 1, total[size : size + 1], first_ref[0:1, :])
    stats_ref[...] = jnp.broadcast_to(stats, stats_ref.shape)


def final_kernel(stats_ref, own_ref, ext_ref, second_ref, weights_ref, coverage_ref):
    stats = stats_ref[...]
    count = jnp.sum(lane_of(stats, 3), axis=0, keepdims=True)
    average_one = jnp.sum(lane_of(stats, 0), axis=0, keepdims=True) / count
    ratio = average_one / lane_of(stats, 2)
    average_two = jnp.sum(lane_of(stats, 1) * ratio * ratio, axis=0, keepdims=True) / count
    blk_g = own_ref.shape[0]
    owns, biases = halves(own_ref[...]), halves(ext_ref[0:blk_g, :])
    for h in range(2):
        rows = pl.ds(h, blk_g, stride=2)
        kept = owns[h] > 0.0
        total = second_ref[rows, :] * average_one
        coverage_ref[rows, :] = (biases[h] * average_one) * total
        weights_ref[rows, :] = jnp.where(kept, average_two / jnp.where(kept, total, 1.0), 0.0)


def call(kernel, ins, outs, scratch=(), cost=None, limit=16):
    return pl.pallas_call(
        kernel,
        in_specs=list(ins),
        out_shape=[jax.ShapeDtypeStruct(s, d) for s, d, _ in outs],
        out_specs=[spec for _, _, spec in outs],
        scratch_shapes=list(scratch),
        compiler_params=pltpu.CompilerParams(vmem_limit_bytes=limit * 1024 * 1024),
        cost_estimate=cost and pl.CostEstimate(flops=cost, bytes_accessed=cost, transcendentals=0),
    )


def floats(*shape):
    return (shape, F32, VMEM)


def exchange(block, axis):
    return lax.all_to_all(block, axis, 0, 0, tiled=True)


def swap_cores(block):
    return lax.ppermute(block, "core", [(0, 1), (1, 0)])


def shards(band, trans, rows_at, cols_at, trans_count, masked):
    blk_dev, spans, width, _ = band.shape
    tiles = trans.shape[0]
    replicas = lax.axis_size("rep")
    chips = lax.axis_size("chip")
    blk_g = blk_dev * replicas
    own_like = floats(blk_g, width)
    send_like = floats(chips * 2 * blk_g, LANES)
    share_like = floats(2 * replicas, blk_g, width)
    cols_scr = pltpu.VMEM((width, LANES), F32)
    wide_scr = pltpu.VMEM((16, width), F32)
    flat_scr = pltpu.VMEM((2 * blk_g, LANES), F32)
    half_scr = pltpu.VMEM((2 * spans - 2, LANES), F32)
    info_scr = [pltpu.SMEM((24,), I32), pltpu.SemaphoreType.DMA(())]
    fill_scr = [cols_scr, wide_scr, flat_scr, half_scr]
    masked, cols_at, rows_at, band, trans = (
        pltpu.with_memory_space_constraint(x, pltpu.HBM)
        for x in (masked.reshape(2 * blk_g, LANES), cols_at, rows_at, band, trans)
    )
    own, info, send, part, band, trans = pl.pallas_call(
        first_kernel,
        in_specs=[SMEM] + [HBM] * 5,
        out_shape=[
            jax.ShapeDtypeStruct((blk_g, width), F32),
            jax.ShapeDtypeStruct((24,), I32),
            jax.ShapeDtypeStruct((chips * 2 * blk_g, LANES), F32),
            jax.ShapeDtypeStruct((blk_g, width), F32),
            pltpu.VMEM(band.shape, F32),
            pltpu.VMEM(trans.shape, F32),
        ],
        out_specs=[VMEM, SMEM, VMEM, VMEM, VMEM, VMEM],
        scratch_shapes=[
            pltpu.VMEM((2 * blk_g, LANES), I32),
            pltpu.SMEM((tiles,), I32),
            pltpu.SMEM((tiles,), I32),
            pltpu.SemaphoreType.DMA((3,)),
            pltpu.SemaphoreType.DMA((tiles + blk_dev,)),
            flat_scr,
        ] + fill_scr,
        compiler_params=pltpu.CompilerParams(vmem_limit_bytes=16 * 1024 * 1024),
    )(trans_count, masked, cols_at, rows_at, band, trans)
    got = exchange(send.reshape(chips, 1, 2 * blk_g * LANES), "chip").reshape(send.shape)
    mate = swap_cores(got)
    share, code = call(
        meet_kernel,
        [VMEM, VMEM, VMEM, VMEM, ANY, VMEM, VMEM],
        [share_like, floats(2, chips, LANES)],
        info_scr + [wide_scr, cols_scr, half_scr],
    )(own, part, got, mate, info, band, trans)
    shares = exchange(share, LOCAL)
    ext, first, send, part = call(
        second_kernel,
        [VMEM, VMEM, ANY, VMEM, VMEM],
        [floats(2 * blk_g, width), floats(8, LANES), floats(STEP * chips, LANES),
         floats(2 * blk_g, width)],
        info_scr + [cols_scr, wide_scr, half_scr, half_scr],
    )(shares, code, info, band, trans)
    got = exchange(send.reshape(chips, 1, STEP * LANES), "chip").reshape(send.shape)
    (share,) = call(
        third_kernel,
        [VMEM, VMEM, VMEM, VMEM, VMEM, ANY, VMEM, VMEM],
        [floats(2 * replicas * SHARE, LANES)],
        info_scr + [wide_scr, cols_scr, half_scr],
    )(code, got, ext, part, first, info, band, trans)
    shares = exchange(share.reshape(2 * replicas, 1, SHARE * LANES), LOCAL).reshape(share.shape)
    second, stats = call(
        stats_kernel, [VMEM, VMEM], [floats(2 * blk_g, LANES), floats(chips, LANES)]
    )(shares, first)
    stats = exchange(stats, "chip")
    weights, coverage = call(
        final_kernel, [VMEM] * 4, [floats(2 * blk_g, LANES)] * 2
    )(stats, own, ext, second)
    return (weights.reshape(-1), coverage.reshape(-1))


GENOME = ("chip", "core")
LOCAL = ("core", "rep")
STEP = 10
SHARE = 18


def solution(mesh):
    names = mesh.axis_names
    groups, replicas = (mesh.shape[name] for name in ("genome", "rep"))
    assert names == ("genome", "rep")
    devices = mesh.devices.reshape(groups // 2, 2, replicas)
    split = Mesh(devices, GENOME + ("rep",))
    every = P(GENOME + ("rep",))
    out_specs = (P(GENOME), P(GENOME))
    return jax.shard_map(
        shards, mesh=split, in_specs=(every,) * 5 + (P(GENOME),), out_specs=out_specs, check_vma=False
    )
```
